1024 devices in a mesh: row: 8 (over x), col: 8 (over z), layer: 16 (over y, core).
Axes of the slice: x: 8, y: 8, z: 8, core: 2. Of those that a mesh axis runs over, the one named last changes fastest.
Arguments:
- a_blocks: bfloat16 [2048, 128, 128], P(('row', 'col', 'layer')), may hold values from -0.25 to 0.25
- a_slot: int32 [2048], P(('row', 'col', 'layer')), may hold values from 0 to 63, as said below
- b_blocks: bfloat16 [1024, 128, 128], P(('row', 'col', 'layer')), may hold values from -6 to 6
- b_slot: int32 [1024], P(('row', 'col', 'layer')), may hold values from 0 to 31, as said below
- c_mask: int32 [128, 64], P('row', 'col'), may hold values from 0 to 1, as said below
Outputs:
- product: float32 [16384, 8192], P(('row', 'layer'), 'col')
The draws below stay inside these ranges and needn't reach their ends.
Inputs may be any that keep to these rules, and one draw needn't show every extreme that they name: `a_slot`: within each row panel r and inner slice l the 16 slots of A are distinct. `b_slot`: within each column panel c and inner slice l the 8 slots of B are distinct. `c_mask`: every block row has exactly 4 ones in each column panel of 8 block columns.
All inputs are finite; a program needn't handle non-finite values.
Results may differ from the reference program's by a relative error of at most 0.0003.
Values may be sent and summed in bfloat16 or wider, within the bound.
A program may use at most 32 MiB of HBM per device.

```python
import jax
import jax.numpy as jnp

BS = 128
MBP = 16
KBL = 4
NBP = 8
NA_DEV = 2
NB_DEV = 1
MB = 128
KB = 64
NB = 64
NAE = 2048
NBE = 1024
N_ROW = 8
N_COL = 8
N_LAYER = 16


def draw_a_slot(key, part):
    key = jax.random.fold_in(key, 11)
    keys = jax.random.split(key, N_ROW * N_LAYER)
    perms = jax.vmap(lambda k: jax.random.permutation(k, MBP * KBL))(keys)
    taken = perms[:, :N_COL * NA_DEV].reshape(N_ROW, N_LAYER, N_COL, NA_DEV)
    return taken.transpose(0, 2, 1, 3).reshape(-1).astype(jnp.int32)


def draw_b_slot(key, part):
    key = jax.random.fold_in(key, 23)
    keys = jax.random.split(key, N_COL * N_LAYER)
    perms = jax.vmap(lambda k: jax.random.permutation(k, KBL * NBP))(keys)
    taken = perms[:, :N_ROW * NB_DEV].reshape(N_COL, N_LAYER, N_ROW, NB_DEV)
    return taken.transpose(2, 0, 1, 3).reshape(-1).astype(jnp.int32)


def draw_c_mask(key, part):
    key = jax.random.fold_in(key, 37)
    keys = jax.random.split(key, MB * N_COL)
    perms = jax.vmap(lambda k: jax.random.permutation(k, NBP))(keys)
    return (perms < NBP // 2).astype(jnp.int32).reshape(MB, NB)


def levels(rng, shape, cuts, low, top_value):
    def one(position, parts):
        steps = jax.random.uniform(jax.random.fold_in(jax.random.fold_in(rng, 6), position), (parts,), jnp.float32, low / len(cuts), top_value / len(cuts))
        return jnp.repeat(jnp.exp(steps), shape[position] // parts).reshape((-1,) + (1,) * (len(shape) - position - 1))

    factor_of = one(*cuts[0])
    for cut in cuts[1:]:
        factor_of = factor_of * one(*cut)
    return factor_of


def scatter_about(stream_key, dims, width, limit, pieces=(), held_as=jnp.bfloat16):
    entries = jax.random.normal(stream_key, dims, jnp.float32) * width
    if len(pieces) > 0:
        entries = levels(stream_key, dims, pieces, -0.22, 0.18) * entries
    return jnp.clip(entries, min=-limit, max=limit).astype(held_as)


def setup_inputs(seed: int = 0) -> dict:
    splits = jax.random.split(jax.random.key(seed), 6)
    return {
        "a_blocks": scatter_about(splits[0], (NAE, BS, BS), (BS * KB // 16) ** -0.5, 0.25, ((0, 1024),)),
        "a_slot": draw_a_slot(jax.random.fold_in(splits[5], 71), 0),
        "b_blocks": scatter_about(splits[2], (NBE, BS, BS), 1.0, 6.0, ((0, 1024),)),
        "b_slot": draw_b_slot(jax.random.fold_in(splits[5], 71), 0),
        "c_mask": draw_c_mask(jax.random.fold_in(splits[5], 71), 0),
    }


def reference(a_blocks, a_slot, b_blocks, b_slot, c_mask):
    a_index = (jnp.arange(NAE) // NA_DEV).astype(jnp.int32)
    a_layer = a_index % N_LAYER
    a_row = (a_index // N_LAYER) // N_COL
    row_block = a_row * MBP + a_slot // KBL
    inner_a = a_layer * KBL + a_slot % KBL
    dense_a = jnp.zeros((MB, KB, BS, BS), jnp.bfloat16).at[row_block, inner_a].set(a_blocks)
    a_matrix = dense_a.transpose(0, 2, 1, 3).reshape(MB * BS, KB * BS)
    b_index = (jnp.arange(NBE) // NB_DEV).astype(jnp.int32)
    b_layer = b_index % N_LAYER
    b_col = (b_index // N_LAYER) % N_COL
    inner_b = b_layer * KBL + b_slot // NBP
    col_block = b_col * NBP + b_slot % NBP
    dense_b = jnp.zeros((KB, NB, BS, BS), jnp.bfloat16).at[inner_b, col_block].set(b_blocks)
    b_matrix = dense_b.transpose(0, 2, 1, 3).reshape(KB * BS, NB * BS)
    full = jnp.dot(a_matrix, b_matrix, preferred_element_type=jnp.float32)
    keep = jnp.broadcast_to(c_mask.astype(jnp.float32)[:, None, :, None], (MB, BS, NB, BS))
    return full * keep.reshape(MB * BS, NB * BS)
```

```python
import functools

import jax
import jax.numpy as jnp
from jax import lax
from jax.experimental import pallas as pl
from jax.experimental.pallas import tpu as pltpu
from jax.sharding import PartitionSpec as P

MESH = pl.DeviceIdType.MESH
BS = 128
ROWS = 16
INNER = 4
COLS = 8
KEPT = 4
RING = 8
TOP = 32760.0
TINY = 1e-30


def wait_bytes(ref, sem):
    pltpu.make_async_copy(ref, ref, sem).wait()


def kernel(
    a_in, a_slot, b_in, b_slot, mask, out,
    a_buf, b_buf, a_tab, b_tab, sum_tx, sum_rx, tab_v, tab_s, sel, tx, tx_scale, rx, rx_scale, comp,
    own_sem, a_recv, b_recv, sib_recv, tab_recv, tab_local, a_send, b_send, tab_send, rs_recv, rs_send,
):
    x, z, layer = lax.axis_index("row"), lax.axis_index("col"), lax.axis_index("layer")
    y, core = lax.div(layer, 2), lax.rem(layer, 2)
    other = 1 - core
    sibling = {"layer": y * 2 + other}
    z_next, z_prev = {"col": lax.rem(z + 1, RING)}, {"col": lax.rem(z + RING - 1, RING)}
    x_next, x_prev = {"row": lax.rem(x + 1, RING)}, {"row": lax.rem(x + RING - 1, RING)}
    way = 1 - 2 * core
    y_long = {"layer": lax.rem(y + way + RING, RING) * 2 + core}
    y_short = {"layer": lax.rem(y - way + RING, RING) * 2 + core}

    barrier = pltpu.get_barrier_semaphore()
    for step in range(1, RING):
        pl.semaphore_signal(barrier, inc=1, device_id={"col": lax.rem(z + step, RING)}, device_id_type=MESH)
        pl.semaphore_signal(barrier, inc=1, device_id={"row": lax.rem(x + step, RING)}, device_id_type=MESH)
    for device in (y_long, y_short, sibling):
        pl.semaphore_signal(barrier, inc=1, device_id=device, device_id_type=MESH)

    own_a = core * 16 + z * 2
    own_b = core * 8 + x
    own = [
        pltpu.make_async_copy(a_in, a_buf.at[pl.ds(own_a, 2)], own_sem.at[0]),
        pltpu.make_async_copy(b_in, b_buf.at[pl.ds(own_b, 1)], own_sem.at[1]),
    ]
    for copy in own:
        copy.start()
    lane = lax.broadcasted_iota(jnp.int32, (1, BS), 1)
    first = jnp.where(lane == core * 64 + a_slot[0], own_a + 1, 0)
    a_tab[z] = jnp.where(lane == core * 64 + a_slot[1], own_a + 2, first)
    b_tab[x] = jnp.where(lane == core * 32 + b_slot[0], own_b + 1, 0)
    a_buf[32] = jnp.zeros((BS, BS), jnp.bfloat16)
    b_buf[16] = jnp.zeros((BS, BS), jnp.bfloat16)
    comp[KEPT] = jnp.zeros((BS, BS), jnp.float32)

    pl.semaphore_wait(barrier, 2 * (RING - 1) + 3)

    def push(src, dst, send, recv, device):
        pltpu.make_async_remote_copy(
            src_ref=src, dst_ref=dst, send_sem=send, recv_sem=recv, device_id=device, device_id_type=MESH
        ).start()

    def push_a(src, origin, first, count, way, hop, device):
        push(src, a_buf.at[pl.ds(core * 16 + origin * 2 + first, count)], a_send, a_recv.at[way, hop], device)

    def push_b(src, origin, first, count, way, hop, device):
        push(src, b_buf.at[core * 8 + origin, pl.ds(first, count)], b_send, b_recv.at[way, hop], device)

    def a_part(origin, first, count):
        return a_buf.at[pl.ds(core * 16 + origin * 2 + first, count)]

    def b_part(origin, first, count):
        return b_buf.at[core * 8 + origin, pl.ds(first, count)]

    push_a(a_in, z, 0, 2, 0, 0, z_next)
    push_a(a_in, z, 0, 2, 1, 0, z_prev)
    push_b(b_in.at[0], x, 0, BS, 0, 0, x_next)
    push_b(b_in.at[0], x, 0, BS, 1, 0, x_prev)
    for step in range(1, RING):
        push(a_tab.at[z], a_tab.at[z], tab_send.at[0], tab_recv.at[0], {"col": lax.rem(z + step, RING)})
        push(b_tab.at[x], b_tab.at[x], tab_send.at[1], tab_recv.at[1], {"row": lax.rem(x + step, RING)})
    push(a_in, a_part(z, 0, 2), a_send, sib_recv.at[0], sibling)
    push(b_in.at[0], b_part(x, 0, BS), b_send, sib_recv.at[1], sibling)

    def pick(t, carry):
        count = jnp.int32(0)
        picks = [jnp.int32(0)] * KEPT
        for j in range(COLS):
            bit = mask[t * 2 + core, j]
            for q in range(KEPT):
                picks[q] = picks[q] + jnp.where(count == q, bit * j, 0)
            count = count + bit
        for q in range(KEPT):
            sel[t, q] = picks[q]
        return carry

    lax.fori_loop(0, RING, pick, 0)

    for hop in range(1, 5):
        a_up, a_down = lax.rem(z + RING - hop, RING), lax.rem(z + hop, RING)
        b_up, b_down = lax.rem(x + RING - hop, RING), lax.rem(x + hop, RING)
        a_whole, b_whole = ((0, 2), (0, BS)) if hop < 4 else ((0, 1), (0, BS // 2))
        a_rest, b_rest = ((0, 2), (0, BS)) if hop < 4 else ((1, 1), (BS // 2, BS // 2))
        a_next = ((0, 2), (0, 2)) if hop < 3 else ((0, 1), (1, 1))
        b_next = ((0, BS), (0, BS)) if hop < 3 else ((0, BS // 2), (BS // 2, BS // 2))
        wait_bytes(a_part(a_up, *a_whole), a_recv.at[0, hop - 1])
        if hop < 4:
            push_a(a_part(a_up, *a_next[0]), a_up, *a_next[0], 0, hop, z_next)
        wait_bytes(a_part(a_down, *a_rest), a_recv.at[1, hop - 1])
        if hop < 4:
            push_a(a_part(a_down, *a_next[1]), a_down, *a_next[1], 1, hop, z_prev)
        push(a_part(a_up, *a_whole), a_part(a_up, *a_whole), a_send, sib_recv.at[0], sibling)
        push(a_part(a_down, *a_rest), a_part(a_down, *a_rest), a_send, sib_recv.at[0], sibling)
        wait_bytes(b_part(b_up, *b_whole), b_recv.at[0, hop - 1])
        if hop < 4:
            push_b(b_part(b_up, *b_next[0]), b_up, *b_next[0], 0, hop, x_next)
        wait_bytes(b_part(b_down, *b_rest), b_recv.at[1, hop - 1])
        if hop < 4:
            push_b(b_part(b_down, *b_next[1]), b_down, *b_next[1], 1, hop, x_prev)
        push(b_part(b_up, *b_whole), b_part(b_up, *b_whole), b_send, sib_recv.at[1], sibling)
        push(b_part(b_down, *b_rest), b_part(b_down, *b_rest), b_send, sib_recv.at[1], sibling)
        if hop == 2:
            wait_bytes(a_tab.at[pl.ds(0, RING - 1)], tab_recv.at[0])
            wait_bytes(b_tab.at[pl.ds(0, RING - 1)], tab_recv.at[1])
            sum_tx[0] = jnp.max(a_tab[...], axis=0)
            sum_tx[1] = jnp.max(b_tab[...], axis=0)
            push(sum_tx, sum_rx, tab_send.at[2], tab_recv.at[2], sibling)
        if hop == 3:
            wait_bytes(sum_rx, tab_recv.at[2])
            both = jnp.maximum(sum_tx[...], sum_rx[...])
            tab_v[0] = jnp.where(both[0] > 0, both[0] - 1, 32)
            tab_v[1] = jnp.where(both[1] > 0, both[1] - 1, 16)
            pltpu.make_async_copy(tab_v, tab_s, tab_local).start()
    pltpu.make_async_copy(tab_v, tab_s, tab_local).wait()
    for copy in own:
        copy.wait()
    wait_bytes(a_buf.at[pl.ds(other * 16, 16)], sib_recv.at[0])
    wait_bytes(b_buf.at[pl.ds(other * 8, 8)], sib_recv.at[1])

    slices = [(s, kk) for s in range(2) for kk in range(INNER)]

    def partial(t):
        row = t * 2 + core
        left = jnp.concatenate([a_buf[tab_s[0, 0, s * 64 + row * INNER + kk]] for s, kk in slices], axis=1)
        sums = []
        for p in range(KEPT // 2):
            right = jnp.concatenate(
                [
                    jnp.concatenate(
                        [b_buf[tab_s[1, 0, s * 32 + kk * COLS + sel[t, 2 * p + q]]] for q in range(2)], axis=1
                    )
                    for s, kk in slices
                ],
                axis=0,
            )
            sums.append(jnp.dot(left, right, preferred_element_type=jnp.float32))
        return sums

    def received(slot, p):
        wait_bytes(rx.at[slot, p], rs_recv.at[slot, p, 0])
        wait_bytes(rx_scale.at[slot, p], rs_recv.at[slot, p, 1])
        return rx[slot, p].astype(jnp.int32).astype(jnp.float32) * rx_scale[slot, p]

    def send(slot, p, value, device):
        top = jnp.maximum(jnp.max(jnp.abs(value), axis=0, keepdims=True), TINY)
        tx_scale[slot, p] = top * (1.0 / TOP)
        tx[slot, p] = jnp.round(value * (TOP / top)).astype(jnp.int32).astype(jnp.int16)
        push(tx_scale.at[slot, p], rx_scale.at[slot, p], rs_send.at[slot, p, 1], rs_recv.at[slot, p, 1], device)
        push(tx.at[slot, p], rx.at[slot, p], rs_send.at[slot, p, 0], rs_recv.at[slot, p, 0], device)

    for hop in range(4):
        t = lax.rem(y + way * (4 - hop) + RING, RING)
        sums = partial(t)
        for p in range(KEPT // 2):
            value = sums[p] if hop == 0 else sums[p] + received(hop - 1, p)
            send(hop, p, value, y_long)
        if hop < 3:
            t = lax.rem(y - way * (3 - hop) + RING, RING)
            sums = partial(t)
            for p in range(KEPT // 2):
                value = sums[p] if hop == 0 else sums[p] + received(3 + hop, p)
                send(4 + hop, p, value, y_short)
    sums = partial(y)
    for p in range(KEPT // 2):
        value = sums[p] + received(6, p) + received(3, p)
        for q in range(2):
            comp[2 * p + q] = value[:, q * BS : (q + 1) * BS]
    count = jnp.int32(0)
    for j in range(COLS):
        bit = mask[layer, j]
        out[:, j * BS : (j + 1) * BS] = comp[jnp.where(bit == 1, count, KEPT)]
        count = count + bit

    wait_bytes(a_buf.at[pl.ds(0, 30)], a_send)
    wait_bytes(b_buf.at[pl.ds(0, 15)], b_send)
    wait_bytes(a_tab.at[pl.ds(0, RING - 1)], tab_send.at[0])
    wait_bytes(b_tab.at[pl.ds(0, RING - 1)], tab_send.at[1])
    wait_bytes(sum_tx, tab_send.at[2])
    for slot in range(7):
        for p in range(KEPT // 2):
            wait_bytes(tx.at[slot, p], rs_send.at[slot, p, 0])
            wait_bytes(tx_scale.at[slot, p], rs_send.at[slot, p, 1])


def on_device(a_blocks, a_slot, b_blocks, b_slot, c_mask):
    vmem, smem, dma = pltpu.VMEM, pltpu.SMEM, pltpu.SemaphoreType.DMA
    any_space = pl.BlockSpec(memory_space=pl.ANY)
    scalars = pl.BlockSpec(memory_space=smem)
    return pl.pallas_call(
        kernel,
        out_shape=jax.ShapeDtypeStruct((BS, COLS * BS), jnp.float32),
        in_specs=[any_space, scalars, any_space, scalars, scalars],
        out_specs=pl.BlockSpec(memory_space=vmem),
        scratch_shapes=[
            vmem((33, BS, BS), jnp.bfloat16),
            vmem((17, BS, BS), jnp.bfloat16),
            vmem((RING, 1, BS), jnp.int32),
            vmem((RING, 1, BS), jnp.int32),
            vmem((2, 1, BS), jnp.int32),
            vmem((2, 1, BS), jnp.int32),
            vmem((2, 1, BS), jnp.int32),
            smem((2, 1, BS), jnp.int32),
            smem((RING, KEPT), jnp.int32),
            vmem((7, 2, BS, 2 * BS), jnp.int16),
            vmem((7, 2, 1, 2 * BS), jnp.float32),
            vmem((7, 2, BS, 2 * BS), jnp.int16),
            vmem((7, 2, 1, 2 * BS), jnp.float32),
            vmem((KEPT + 1, BS, BS), jnp.float32),
            dma((2,)),
            dma((2, 4)),
            dma((2, 4)),
            dma((2,)),
            dma((3,)),
            dma(()),
            dma(()),
            dma(()),
            dma((3,)),
            dma((7, 2, 2)),
            dma((7, 2, 2)),
        ],
        compiler_params=pltpu.CompilerParams(
            collective_id=0, has_side_effects=True, vmem_limit_bytes=40 * 1024 * 1024
        ),
    )(a_blocks, a_slot, b_blocks, b_slot, c_mask)


def solution(mesh):
    in_specs = (
        P(("row", "col", "layer"), None, None),
        P(("row", "col", "layer")),
        P(("row", "col", "layer"), None, None),
        P(("row", "col", "layer")),
        P("row", "col"),
    )
    out_specs = P(("row", "layer"), "col")
    return jax.shard_map(on_device, mesh=mesh, in_specs=in_specs, out_specs=out_specs, check_vma=False)
```

```python
import functools

import jax
import jax.numpy as jnp
from jax import lax
from jax.experimental import pallas as pl
from jax.experimental.pallas import tpu as pltpu
from jax.sharding import PartitionSpec as P

MESH = pl.DeviceIdType.MESH
BS = 128
ROWS = 16
INNER = 4
COLS = 8
KEPT = 4
RING = 8
TOP = 32760.0
TINY = 1e-30


def wait_bytes(ref, sem):
    pltpu.make_async_copy(ref, ref, sem).wait()


def kernel(
    a_in, a_slot_in, b_in, b_slot_in, mask_in, out,
    a_slot, b_slot, mask, a_buf, b_buf, a_tab, b_tab, tab_v, tab_s, sel, tx, tx_scale, rx, rx_scale, comp,
    in_sem, own_sem, z_in, x_in, y_in, sib_in, a_recv, b_recv, sib_recv, tab_recv, tab_local,
    a_send, b_send, tab_send, rs_recv, rs_send,
):
    x, z, layer = lax.axis_index("row"), lax.axis_index("col"), lax.axis_index("layer")
    y, core = lax.div(layer, 2), lax.rem(layer, 2)
    other = 1 - core
    twin = y * 2 + other
    sibling = {"layer": twin}
    y_up, y_down = lax.rem(y + 1, RING), lax.rem(y + RING - 1, RING)
    way = 1 - 2 * core
    y_long = {"layer": lax.rem(y + way + RING, RING) * 2 + core}
    y_short = {"layer": lax.rem(y - way + RING, RING) * 2 + core}

    loads = [
        pltpu.make_async_copy(a_slot_in, a_slot, in_sem.at[0]),
        pltpu.make_async_copy(b_slot_in, b_slot, in_sem.at[1]),
        pltpu.make_async_copy(mask_in, mask, in_sem.at[2]),
    ]
    for copy in loads:
        copy.start()

    barrier = pltpu.get_barrier_semaphore()

    def signal(sem, device):
        pl.semaphore_signal(sem, inc=1, device_id=device, device_id_type=MESH)

    for p in range(1, RING):

        @pl.when(p > z)
        def _():
            signal(barrier, {"col": p})
            signal(barrier, {"col": p, "layer": twin})

        @pl.when(p > x)
        def _():
            signal(barrier, {"row": p})
            signal(barrier, {"row": p, "layer": twin})

    for peer in (y_up, y_down):

        @pl.when(peer > y)
        def _():
            signal(barrier, {"layer": peer * 2 + core})

    @pl.when(core == 0)
    def _():
        signal(barrier, sibling)

    own_a = core * 16 + z * 2
    own_b = core * 8 + x
    own = [
        pltpu.make_async_copy(a_in, a_buf.at[pl.ds(own_a, 2)], own_sem.at[0]),
        pltpu.make_async_copy(b_in, b_buf.at[pl.ds(own_b, 1)], own_sem.at[1]),
    ]
    for copy in own:
        copy.start()
    lower_y = jnp.where(y_up < y, 1, 0) + jnp.where(y_down < y, 1, 0)
    n_lower = 2 * z + 2 * x + lower_y + core

    @pl.when(n_lower > 0)
    def _():
        pl.semaphore_wait(barrier, n_lower)

    def push(src, dst, send, recv, device):
        pltpu.make_async_remote_copy(
            src_ref=src, dst_ref=dst, send_sem=send, recv_sem=recv, device_id=device, device_id_type=MESH
        ).start()

    def push_a(p):
        push(a_in, a_buf.at[pl.ds(own_a, 2)], a_send, a_recv.at[z], {"col": p})

    def push_b(p):
        push(b_in, b_buf.at[pl.ds(own_b, 1)], b_send, b_recv.at[x], {"row": p})

    def push_a_tab(device):
        row = a_tab.at[core * 8 + z]
        push(row, row, tab_send.at[0], tab_recv.at[0], device)

    def push_b_tab(device):
        row = b_tab.at[core * 8 + x]
        push(row, row, tab_send.at[1], tab_recv.at[1], device)

    for p in range(RING - 1):

        @pl.when(p < z)
        def _():
            push_a(p)

    for p in range(RING - 1):

        @pl.when(p < z)
        def _():
            signal(z_in.at[core, z], {"col": p})
            signal(z_in.at[core, z], {"col": p, "layer": twin})

        @pl.when(p < x)
        def _():
            signal(x_in.at[core, x], {"row": p})
            signal(x_in.at[core, x], {"row": p, "layer": twin})

    @pl.when(y_up < y)
    def _():
        signal(y_in.at[1], {"layer": y_up * 2 + core})

    @pl.when(y_down < y)
    def _():
        signal(y_in.at[0], {"layer": y_down * 2 + core})

    @pl.when(core == 1)
    def _():
        signal(sib_in, sibling)

    for copy in loads:
        copy.wait()
    lane = lax.broadcasted_iota(jnp.int32, (1, BS), 1)
    first = jnp.where(lane == core * 64 + a_slot[0], own_a + 1, 0)
    a_tab[core * 8 + z] = jnp.where(lane == core * 64 + a_slot[1], own_a + 2, first)
    b_tab[core * 8 + x] = jnp.where(lane == core * 32 + b_slot[0], own_b + 1, 0)

    for p in range(RING - 1):

        @pl.when(p < z)
        def _():
            push_a_tab({"col": p})
            push_a_tab({"col": p, "layer": twin})

    for p in range(RING - 1):

        @pl.when(p < x)
        def _():
            push_b(p)
            push_b_tab({"row": p})
            push_b_tab({"row": p, "layer": twin})

    @pl.when(core == 0)
    def _():
        pl.semaphore_wait(sib_in, 1)

    push(a_in, a_buf.at[pl.ds(own_a, 2)], a_send, sib_recv.at[0], sibling)
    push(b_in, b_buf.at[pl.ds(own_b, 1)], b_send, sib_recv.at[1], sibling)
    push_a_tab(sibling)
    push_b_tab(sibling)

    a_buf[32] = jnp.zeros((BS, BS), jnp.bfloat16)
    b_buf[16] = jnp.zeros((BS, BS), jnp.bfloat16)
    comp[KEPT] = jnp.zeros((BS, BS), jnp.float32)

    for p in range(1, RING):

        @pl.when(p > x)
        def _():
            pl.semaphore_wait(x_in.at[core, p], 1)
            pl.semaphore_wait(x_in.at[other, p], 1)
            push_b(p)
            push_b_tab({"row": p})
            push_b_tab({"row": p, "layer": twin})

    def pick(t, carry):
        count = jnp.int32(0)
        picks = [jnp.int32(0)] * KEPT
        for j in range(COLS):
            bit = mask[j, t * 2 + core]
            for q in range(KEPT):
                picks[q] = picks[q] + jnp.where(count == q, bit * j, 0)
            count = count + bit
        for q in range(KEPT):
            sel[t, q] = picks[q]
        return carry

    lax.fori_loop(0, RING, pick, 0)

    for p in range(1, RING):

        @pl.when(p > z)
        def _():
            pl.semaphore_wait(z_in.at[core, p], 1)
            pl.semaphore_wait(z_in.at[other, p], 1)
            push_a(p)
            push_a_tab({"col": p})
            push_a_tab({"col": p, "layer": twin})

    @pl.when(y_up > y)
    def _():
        pl.semaphore_wait(y_in.at[0], 1)

    @pl.when(y_down > y)
    def _():
        pl.semaphore_wait(y_in.at[1], 1)

    for p in range(RING):

        @pl.when(p != x)
        def _():
            block = b_buf.at[pl.ds(core * 8 + p, 1)]
            wait_bytes(block, b_recv.at[p])
            push(block, block, b_send, sib_recv.at[1], sibling)

    for p in range(RING):

        @pl.when(p != z)
        def _():
            blocks = a_buf.at[pl.ds(core * 16 + p * 2, 2)]
            wait_bytes(blocks, a_recv.at[p])
            push(blocks, blocks, a_send, sib_recv.at[0], sibling)

    wait_bytes(a_tab.at[pl.ds(0, 15)], tab_recv.at[0])
    wait_bytes(b_tab.at[pl.ds(0, 15)], tab_recv.at[1])
    a_at, b_at = jnp.max(a_tab[...], axis=0), jnp.max(b_tab[...], axis=0)
    tab_v[0] = jnp.where(a_at > 0, a_at - 1, 32)
    tab_v[1] = jnp.where(b_at > 0, b_at - 1, 16)
    to_scalars = pltpu.make_async_copy(tab_v, tab_s, tab_local)
    to_scalars.start()
    for copy in own:
        copy.wait()
    to_scalars.wait()
    wait_bytes(a_buf.at[pl.ds(other * 16, 16)], sib_recv.at[0])
    wait_bytes(b_buf.at[pl.ds(other * 8, 8)], sib_recv.at[1])

    slices = [(s, kk) for s in range(2) for kk in range(INNER)]

    def partial(t):
        row = t * 2 + core
        left = jnp.concatenate([a_buf[tab_s[0, 0, s * 64 + row * INNER + kk]] for s, kk in slices], axis=1)
        sums = []
        for p in range(KEPT // 2):
            right = jnp.concatenate(
                [
                    jnp.concatenate(
                        [b_buf[tab_s[1, 0, s * 32 + kk * COLS + sel[t, 2 * p + q]]] for q in range(2)], axis=1
                    )
                    for s, kk in slices
                ],
                axis=0,
            )
            both = jnp.dot(left, right, preferred_element_type=jnp.float32)
            sums += [both[:, :BS], both[:, BS:]]
        return sums

    def received(slot, q):
        wait_bytes(rx_scale.at[slot, q], rs_recv.at[slot, q, 1])
        wait_bytes(rx.at[slot, q], rs_recv.at[slot, q, 0])
        return rx[slot, q].astype(jnp.int32).astype(jnp.float32) * rx_scale[slot, q]

    def send(slot, q, value, device):
        top = jnp.maximum(jnp.max(jnp.abs(value), axis=0, keepdims=True), TINY)
        tx_scale[slot, q] = top * (1.0 / TOP)
        tx[slot, q] = jnp.round(value * (TOP / top)).astype(jnp.int32).astype(jnp.int16)
        push(tx_scale.at[slot, q], rx_scale.at[slot, q], rs_send.at[slot, q, 1], rs_recv.at[slot, q, 1], device)
        push(tx.at[slot, q], rx.at[slot, q], rs_send.at[slot, q, 0], rs_recv.at[slot, q, 0], device)

    for hop in range(4):
        t = lax.rem(y + way * (4 - hop) + RING, RING)
        sums = partial(t)
        for q in range(KEPT):
            send(hop, q, sums[q] if hop == 0 else sums[q] + received(hop - 1, q), y_long)
        if hop < 3:
            t = lax.rem(y - way * (3 - hop) + RING, RING)
            sums = partial(t)
            for q in range(KEPT):
                send(4 + hop, q, sums[q] if hop == 0 else sums[q] + received(3 + hop, q), y_short)
    sums = partial(y)
    for q in range(KEPT):
        comp[q] = sums[q] + received(6, q) + received(3, q)
    count = jnp.int32(0)
    for j in range(COLS):
        bit = mask[j, layer]
        out[:, j * BS : (j + 1) * BS] = comp[jnp.where(bit == 1, count, KEPT)]
        count = count + bit

    wait_bytes(a_buf.at[pl.ds(0, 30)], a_send)
    wait_bytes(b_buf.at[pl.ds(0, 15)], b_send)
    wait_bytes(a_tab.at[pl.ds(0, 15)], tab_send.at[0])
    wait_bytes(b_tab.at[pl.ds(0, 15)], tab_send.at[1])
    for slot in range(7):
        for q in range(KEPT):
            wait_bytes(tx.at[slot, q], rs_send.at[slot, q, 0])
            wait_bytes(tx_scale.at[slot, q], rs_send.at[slot, q, 1])


def on_device(a_blocks, a_slot, b_blocks, b_slot, c_mask):
    vmem, smem, dma = pltpu.VMEM, pltpu.SMEM, pltpu.SemaphoreType.DMA
    regular = pltpu.SemaphoreType.REGULAR
    return pl.pallas_call(
        kernel,
        out_shape=jax.ShapeDtypeStruct((BS, COLS * BS), jnp.float32),
        in_specs=[pl.BlockSpec(memory_space=pl.ANY)] * 5,
        out_specs=pl.BlockSpec(memory_space=vmem),
        scratch_shapes=[
            smem((2,), jnp.int32),
            smem((1,), jnp.int32),
            smem((COLS, ROWS), jnp.int32),
            vmem((33, BS, BS), jnp.bfloat16),
            vmem((17, BS, BS), jnp.bfloat16),
            vmem((2 * RING, 1, BS), jnp.int32),
            vmem((2 * RING, 1, BS), jnp.int32),
            vmem((2, 1, BS), jnp.int32),
            smem((2, 1, BS), jnp.int32),
            smem((RING, KEPT), jnp.int32),
            vmem((7, KEPT, BS, BS), jnp.int16),
            vmem((7, KEPT, 1, BS), jnp.float32),
            vmem((7, KEPT, BS, BS), jnp.int16),
            vmem((7, KEPT, 1, BS), jnp.float32),
            vmem((KEPT + 1, BS, BS), jnp.float32),
            dma((3,)),
            dma((2,)),
            regular((2, RING)),
            regular((2, RING)),
            regular((2,)),
            regular(()),
            dma((RING,)),
            dma((RING,)),
            dma((2,)),
            dma((2,)),
            dma(()),
            dma(()),
            dma(()),
            dma((2,)),
            dma((7, KEPT, 2)),
            dma((7, KEPT, 2)),
        ],
        compiler_params=pltpu.CompilerParams(
            collective_id=0, has_side_effects=True, vmem_limit_bytes=56 * 1024 * 1024
        ),
    )(a_blocks, a_slot, b_blocks, b_slot, c_mask.T)


def solution(mesh):
    in_specs = (
        P(("row", "col", "layer"), None, None),
        P(("row", "col", "layer")),
        P(("row", "col", "layer"), None, None),
        P(("row", "col", "layer")),
        P("row", "col"),
    )
    out_specs = P(("row", "layer"), "col")
    return jax.shard_map(on_device, mesh=mesh, in_specs=in_specs, out_specs=out_specs, check_vma=False)
```

```python
import functools

import jax
import jax.numpy as jnp
from jax import lax
from jax.experimental import pallas as pl
from jax.experimental.pallas import tpu as pltpu
from jax.sharding import PartitionSpec as P

MESH = pl.DeviceIdType.MESH
BS = 128
ROWS = 16
INNER = 4
COLS = 8
KEPT = 4
RING = 8
TOP = 32760.0
TINY = 1e-30


X_ORDER = Y_ORDER = (0, 1, 2, 3, 7, 6, 5, 4)


def place(index, order):
    found = jnp.int32(0)
    for n, p in enumerate(order):
        found = jnp.where(index == p, n, found)
    return found


def member(n, order):
    found = jnp.int32(0)
    for m, p in enumerate(order):
        found = jnp.where(n == m, p, found)
    return found


def wait_bytes(ref, sem):
    pltpu.make_async_copy(ref, ref, sem).wait()


def kernel(
    a_in, a_slot_in, b_in, b_slot_in, mask_in, out,
    a_slot, b_slot, mask, a_buf, b_buf, a_tab, b_tab, tab_v, tab_s, sel, tx, tx_scale, rx, rx_scale, comp,
    in_sem, own_sem, z_in, x_in, y_in, sib_in, a_recv, b_recv, sib_recv, tab_recv, tab_local,
    a_send, b_send, tab_send, rs_recv, rs_send,
):
    x, z, layer = lax.axis_index("row"), lax.axis_index("col"), lax.axis_index("layer")
    y, core = lax.div(layer, 2), lax.rem(layer, 2)
    other = 1 - core
    twin = y * 2 + other
    sibling = {"layer": twin}
    y_up, y_down = lax.rem(y + 1, RING), lax.rem(y + RING - 1, RING)
    way = 1 - 2 * core
    y_long = {"layer": lax.rem(y + way + RING, RING) * 2 + core}
    y_short = {"layer": lax.rem(y - way + RING, RING) * 2 + core}

    loads = [
        pltpu.make_async_copy(a_slot_in, a_slot, in_sem.at[0]),
        pltpu.make_async_copy(b_slot_in, b_slot, in_sem.at[1]),
        pltpu.make_async_copy(mask_in, mask, in_sem.at[2]),
    ]
    for copy in loads:
        copy.start()

    barrier = pltpu.get_barrier_semaphore()

    def flag(condition):
        return jnp.where(condition, 1, 0)

    def signal(sem, device):
        pl.semaphore_signal(sem, inc=1, device_id=device, device_id_type=MESH)

    at_x, at_y, at_z, at_core = flag(x == 0), flag(y == 0), flag(z == 0), flag(core == 0)
    is_zero = at_x * at_y * at_z * at_core
    x_place, y_place = place(x, X_ORDER), place(y, Y_ORDER)
    z_rank, x_rank, y_rank = z + 8 * is_zero, x_place + 8 * is_zero, y_place + 8 * is_zero
    core_rank = core + 2 * is_zero
    sib_rank = other + 2 * (at_x * at_y * at_z * core)

    def z_peer(p, twin):
        return p + (8 * (at_x * at_y * (core if twin else at_core)) if p == 0 else 0)

    def x_peer(p, twin):
        return X_ORDER.index(p) + (8 * (at_y * at_z * (core if twin else at_core)) if p == 0 else 0)

    def y_peer(p):
        return place(p, Y_ORDER) + 8 * (at_x * at_z * at_core * flag(p == 0))

    def after(peer, me, fn, *args):
        pl.when(peer > me)(functools.partial(fn, *args))

    def before(peer, me, fn, *args):
        pl.when(peer < me)(functools.partial(fn, *args))

    def ring(place, own_zero, twin_zero):
        spot = lax.rem(place - own_zero + RING, RING)
        turn = twin_zero * flag(place > 0)
        twin_spot = place - turn

        def over(first, end, shift, fn):
            def step(n, carry):
                fn(lax.rem(n + shift, RING))
                return carry

            lax.fori_loop(first, end, step, 0)

        def all_before(fn):
            over(0, spot, own_zero, fn)

        def all_after(fn):
            over(spot + 1, RING, own_zero, fn)

        def twins_before(fn):
            over(is_zero, twin_spot + 8 * is_zero, turn, fn)

        def twins_after(fn):
            over(twin_spot + 1 + 8 * is_zero, RING, turn, fn)

        return all_before, all_after, twins_before, twins_after

    z_before, z_later, z_twins_before, z_twins_later = ring(z, at_x * at_y * at_core, at_x * at_y * core)
    x_before, x_later, x_twins_before, x_twins_later = ring(x_place, at_y * at_z * at_core, at_y * at_z * core)

    def col(p):
        return {"col": p}

    def col_twin(p):
        return {"col": p, "layer": twin}

    def row(n):
        return {"row": member(n, X_ORDER)}

    def row_twin(n):
        return {"row": member(n, X_ORDER), "layer": twin}

    after(sib_rank, core_rank, signal, barrier, sibling)
    for peer in (y_up, y_down):
        after(y_peer(peer), y_rank, signal, barrier, {"layer": peer * 2 + core})
    x_later(lambda n: signal(barrier, row(n)))
    x_twins_later(lambda n: signal(barrier, row_twin(n)))
    z_later(lambda p: signal(barrier, col(p)))
    z_twins_later(lambda p: signal(barrier, col_twin(p)))

    own_a = core * 16 + z * 2
    own_b = core * 8 + x
    own = [
        pltpu.make_async_copy(a_in, a_buf.at[pl.ds(own_a, 2)], own_sem.at[0]),
        pltpu.make_async_copy(b_in, b_buf.at[pl.ds(own_b, 1)], own_sem.at[1]),
    ]
    for copy in own:
        copy.start()
    z_lower = 2 * z - flag(z > 0) * at_x * at_y
    x_lower = 2 * x_place - flag(x > 0) * at_y * at_z
    y_lower = flag(y_peer(y_up) < y_rank) + flag(y_peer(y_down) < y_rank)
    n_lower = jnp.where(is_zero == 1, 4 * (RING - 1), z_lower + x_lower) + y_lower + flag(sib_rank < core_rank)

    @pl.when(n_lower > 0)
    def _():
        pl.semaphore_wait(barrier, n_lower)

    def push(src, dst, send, recv, device):
        pltpu.make_async_remote_copy(
            src_ref=src, dst_ref=dst, send_sem=send, recv_sem=recv, device_id=device, device_id_type=MESH
        ).start()

    def push_a(p):
        push(a_in, a_buf.at[pl.ds(own_a, 2)], a_send, a_recv.at[z], col(p))

    def push_b(device):
        push(b_in, b_buf.at[pl.ds(own_b, 1)], b_send, b_recv.at[x], device)

    def push_a_tab(device):
        row = a_tab.at[core * 8 + z]
        push(row, row, tab_send.at[0], tab_recv.at[0], device)

    def push_b_tab(device):
        row = b_tab.at[core * 8 + x]
        push(row, row, tab_send.at[1], tab_recv.at[1], device)

    group = lax.div(z, 4)
    is_end = flag(z == 0) + flag(z == 3) + flag(z == 4) + flag(z == 7)
    line_of_zero = at_x * at_y * at_core
    z_inner = {"col": z + 1 - 2 * lax.rem(z, 2)}

    def push_a_if_direct(p):
        near = flag(lax.div(p, 4) == group)
        end = flag(p == 0) + flag(p == 3) + flag(p == 4) + flag(p == 7)
        extra = flag(z == 7) * flag(p == 1)
        pl.when(near + end + extra > 0)(functools.partial(push_a, p))

    z_before(push_a_if_direct)

    for copy in loads[:2]:
        copy.wait()
    lane = lax.broadcasted_iota(jnp.int32, (1, BS), 1)
    first = jnp.where(lane == core * 64 + a_slot[0], own_a + 1, 0)
    a_tab[core * 8 + z] = jnp.where(lane == core * 64 + a_slot[1], own_a + 2, first)
    b_tab[core * 8 + x] = jnp.where(lane == core * 32 + b_slot[0], own_b + 1, 0)

    z_before(lambda p: push_a_tab(col(p)))
    z_twins_before(lambda p: push_a_tab(col_twin(p)))
    z_before(lambda p: signal(z_in.at[core, z], col(p)))
    z_twins_before(lambda p: signal(z_in.at[core, z], col_twin(p)))
    x_before(lambda n: push_b(row(n)))
    x_before(lambda n: push_b_tab(row(n)))
    x_twins_before(lambda n: push_b_tab(row_twin(n)))
    x_before(lambda n: signal(x_in.at[core, x], row(n)))
    x_twins_before(lambda n: signal(x_in.at[core, x], row_twin(n)))

    before(y_peer(y_up), y_rank, signal, y_in.at[1], {"layer": y_up * 2 + core})
    before(y_peer(y_down), y_rank, signal, y_in.at[0], {"layer": y_down * 2 + core})
    before(sib_rank, core_rank, signal, sib_in, sibling)

    @pl.when(sib_rank > core_rank)
    def _():
        pl.semaphore_wait(sib_in, 1)

    push(a_in, a_buf.at[pl.ds(own_a, 2)], a_send, sib_recv.at[0], sibling)
    push(b_in, b_buf.at[pl.ds(own_b, 1)], b_send, sib_recv.at[1], sibling)
    push_a_tab(sibling)
    push_b_tab(sibling)

    a_buf[32] = jnp.zeros((BS, BS), jnp.bfloat16)
    b_buf[16] = jnp.zeros((BS, BS), jnp.bfloat16)
    comp[KEPT] = jnp.zeros((BS, BS), jnp.float32)

    def x_after(p):
        pl.semaphore_wait(x_in.at[core, p], 1)
        push_b({"row": p})
        push_b_tab({"row": p})

    def x_after_twin(p):
        pl.semaphore_wait(x_in.at[other, p], 1)
        push_b_tab({"row": p, "layer": twin})

    for p in X_ORDER[1:] + (0,):

        @pl.when(p != x)
        def _():
            after(x_peer(p, 0), x_rank, x_after, p)
            after(x_peer(p, 1), x_rank, x_after_twin, p)

    loads[2].wait()

    def pick(t, carry):
        count = jnp.int32(0)
        picks = [jnp.int32(0)] * KEPT
        for j in range(COLS):
            bit = mask[j, t * 2 + core]
            for q in range(KEPT):
                picks[q] = picks[q] + jnp.where(count == q, bit * j, 0)
            count = count + bit
        for q in range(KEPT):
            sel[t, q] = picks[q]
        return carry

    lax.fori_loop(0, RING, pick, 0)

    def z_after(p):
        pl.semaphore_wait(z_in.at[core, p], 1)
        push_a_if_direct(p)
        push_a_tab({"col": p})

    def z_after_twin(p):
        pl.semaphore_wait(z_in.at[other, p], 1)
        push_a_tab({"col": p, "layer": twin})

    def offer(peers):
        for p in peers:

            @pl.when(p != z)
            def _():
                after(z_peer(p, 0), z_rank, z_after, p)
                after(z_peer(p, 1), z_rank, z_after_twin, p)

    def share_b():
        for p in range(RING):

            @pl.when(p != x)
            def _():
                block = b_buf.at[pl.ds(core * 8 + p, 1)]
                wait_bytes(block, b_recv.at[p])
                push(block, block, b_send, sib_recv.at[1], sibling)

    def share_a(peers):
        for p in peers:

            @pl.when(p != z)
            def _():
                blocks = a_buf.at[pl.ds(core * 16 + p * 2, 2)]
                wait_bytes(blocks, a_recv.at[p])

                inwards = is_end * flag(group != p // 4)
                if p == 7:
                    inwards = inwards * flag(z != 0)

                @pl.when(inwards == 1)
                def _():
                    push(blocks, blocks, a_send, a_recv.at[p], z_inner)

                push(blocks, blocks, a_send, sib_recv.at[0], sibling)

    forwards = (flag(z == 0) + flag(z == 3)) * (1 - line_of_zero)
    offer((1, 2, 3))

    @pl.when(group == 0)
    def _():
        share_b()
        share_a((1, 2, 3))

    offer((4, 5))

    @pl.when(forwards == 1)
    def _():
        share_a((4,))

    offer((6,))

    @pl.when(forwards == 1)
    def _():
        share_a((5,))

    offer((7, 0))

    @pl.when(y_peer(y_up) > y_rank)
    def _():
        pl.semaphore_wait(y_in.at[0], 1)

    @pl.when(y_peer(y_down) > y_rank)
    def _():
        pl.semaphore_wait(y_in.at[1], 1)

    @pl.when(group == 1)
    def _():
        share_b()
        share_a((1, 2, 3))

    @pl.when(forwards == 0)
    def _():
        share_a((4, 5))

    share_a((6, 7, 0))
    wait_bytes(a_tab.at[pl.ds(0, 15)], tab_recv.at[0])
    wait_bytes(b_tab.at[pl.ds(0, 15)], tab_recv.at[1])
    a_at, b_at = jnp.max(a_tab[...], axis=0), jnp.max(b_tab[...], axis=0)
    tab_v[0] = jnp.where(a_at > 0, a_at - 1, 32)
    tab_v[1] = jnp.where(b_at > 0, b_at - 1, 16)
    to_scalars = pltpu.make_async_copy(tab_v, tab_s, tab_local)
    to_scalars.start()
    for copy in own:
        copy.wait()
    to_scalars.wait()
    wait_bytes(a_buf.at[pl.ds(other * 16, 16)], sib_recv.at[0])
    wait_bytes(b_buf.at[pl.ds(other * 8, 8)], sib_recv.at[1])

    slices = [(s, kk) for s in range(2) for kk in range(INNER)]

    def partial(t):
        row = t * 2 + core
        left = jnp.concatenate([a_buf[tab_s[0, 0, s * 64 + row * INNER + kk]] for s, kk in slices], axis=1)
        sums = []
        for p in range(KEPT // 2):
            right = jnp.concatenate(
                [
                    jnp.concatenate(
                        [b_buf[tab_s[1, 0, s * 32 + kk * COLS + sel[t, 2 * p + q]]] for q in range(2)], axis=1
                    )
                    for s, kk in slices
                ],
                axis=0,
            )
            both = jnp.dot(left, right, preferred_element_type=jnp.float32)
            sums += [both[:, :BS], both[:, BS:]]
        return sums

    def received(slot, q):
        wait_bytes(rx_scale.at[slot, q], rs_recv.at[slot, q, 1])
        wait_bytes(rx.at[slot, q], rs_recv.at[slot, q, 0])
        return rx[slot, q].astype(jnp.int32).astype(jnp.float32) * rx_scale[slot, q]

    def send(slot, q, value, device):
        top = jnp.maximum(jnp.max(jnp.abs(value), axis=0, keepdims=True), TINY)
        tx_scale[slot, q] = top * (1.0 / TOP)
        tx[slot, q] = jnp.round(value * (TOP / top)).astype(jnp.int32).astype(jnp.int16)
        push(tx_scale.at[slot, q], rx_scale.at[slot, q], rs_send.at[1], rs_recv.at[slot, q, 1], device)
        push(tx.at[slot, q], rx.at[slot, q], rs_send.at[2 if slot == 0 else 0], rs_recv.at[slot, q, 0], device)

    for hop in range(4):
        t = lax.rem(y + way * (4 - hop) + RING, RING)
        sums = partial(t)
        for q in range(KEPT):
            send(hop, q, sums[q] if hop == 0 else sums[q] + received(hop - 1, q), y_long)
        if hop < 3:
            t = lax.rem(y - way * (3 - hop) + RING, RING)
            sums = partial(t)
            for q in range(KEPT):
                send(4 + hop, q, sums[q] if hop == 0 else sums[q] + received(3 + hop, q), y_short)
    sums = partial(y)
    for q in range(KEPT):
        comp[q] = sums[q] + received(6, q) + received(3, q)
    count = jnp.int32(0)
    for j in range(COLS):
        bit = mask[j, layer]
        out[:, j * BS : (j + 1) * BS] = comp[jnp.where(bit == 1, count, KEPT)]
        count = count + bit

    wait_bytes(a_buf.at[pl.ds(0, 26)], a_send)

    @pl.when(z == 7)
    def _():
        wait_bytes(a_buf.at[pl.ds(0, 2)], a_send)

    @pl.when(is_end == 1)
    def _():
        wait_bytes(a_buf.at[pl.ds(0, 6)], a_send)

    @pl.when(is_end * flag(z != 0) == 1)
    def _():
        wait_bytes(a_buf.at[pl.ds(0, 2)], a_send)

    wait_bytes(b_buf.at[pl.ds(0, 15)], b_send)
    wait_bytes(a_tab.at[pl.ds(0, 15)], tab_send.at[0])
    wait_bytes(b_tab.at[pl.ds(0, 15)], tab_send.at[1])
    wait_bytes(tx.at[pl.ds(1, 6)], rs_send.at[0])
    wait_bytes(tx_scale, rs_send.at[1])
    wait_bytes(tx.at[0], rs_send.at[2])


def on_device(a_blocks, a_slot, b_blocks, b_slot, c_mask):
    vmem, smem, dma = pltpu.VMEM, pltpu.SMEM, pltpu.SemaphoreType.DMA
    regular = pltpu.SemaphoreType.REGULAR
    operands = (a_blocks, a_slot, b_blocks, b_slot, c_mask.T)
    operands = [operand if operand is b_slot else pltpu.with_memory_space_constraint(operand, pltpu.HBM) for operand in operands]
    return pl.pallas_call(
        kernel,
        out_shape=jax.ShapeDtypeStruct((BS, COLS * BS), jnp.float32),
        in_specs=[pl.BlockSpec(memory_space=pltpu.HBM)] * 5,
        out_specs=pl.BlockSpec(memory_space=vmem),
        scratch_shapes=[
            smem((2,), jnp.int32),
            smem((1,), jnp.int32),
            smem((COLS, ROWS), jnp.int32),
            vmem((33, BS, BS), jnp.bfloat16),
            vmem((17, BS, BS), jnp.bfloat16),
            vmem((2 * RING, 1, BS), jnp.int32),
            vmem((2 * RING, 1, BS), jnp.int32),
            vmem((2, 1, BS), jnp.int32),
            smem((2, 1, BS), jnp.int32),
            smem((RING, KEPT), jnp.int32),
            vmem((7, KEPT, BS, BS), jnp.int16),
            vmem((7, KEPT, 1, BS), jnp.float32),
            vmem((7, KEPT, BS, BS), jnp.int16),
            vmem((7, KEPT, 1, BS), jnp.float32),
            vmem((KEPT + 1, BS, BS), jnp.float32),
            dma((3,)),
            dma((2,)),
            regular((2, RING)),
            regular((2, RING)),
            regular((2,)),
            regular(()),
            dma((RING,)),
            dma((RING,)),
            dma((2,)),
            dma((2,)),
            dma(()),
            dma(()),
            dma(()),
            dma((2,)),
            dma((7, KEPT, 2)),
            dma((3,)),
        ],
        compiler_params=pltpu.CompilerParams(
            collective_id=0, has_side_effects=True, vmem_limit_bytes=40 * 1024 * 1024
        ),
    )(*operands)


def solution(mesh):
    in_specs = (
        P(("row", "col", "layer"), None, None),
        P(("row", "col", "layer")),
        P(("row", "col", "layer"), None, None),
        P(("row", "col", "layer")),
        P("row", "col"),
    )
    out_specs = P(("row", "layer"), "col")
    return jax.shard_map(on_device, mesh=mesh, in_specs=in_specs, out_specs=out_specs, check_vma=False)
```

```python
import functools

import jax
import jax.numpy as jnp
from jax import lax
from jax.experimental import pallas as pl
from jax.experimental.pallas import tpu as pltpu
from jax.sharding import PartitionSpec as P

MESH = pl.DeviceIdType.MESH
BS = 128
ROWS = 16
INNER = 4
COLS = 8
KEPT = 4
RING = 8
TOP = 32760.0
TINY = 1e-30


DIRECT_TO_1, DIRECT_TO_2 = (6, 7), ()
X_ORDER = Y_ORDER = (0, 1, 2, 3, 7, 6, 5, 4)


def place(index, order):
    found = jnp.int32(0)
    for n, p in enumerate(order):
        found = jnp.where(index == p, n, found)
    return found


def member(n, order):
    found = jnp.int32(0)
    for m, p in enumerate(order):
        found = jnp.where(n == m, p, found)
    return found


def wait_bytes(ref, sem):
    pltpu.make_async_copy(ref, ref, sem).wait()


def kernel(
    a_in, a_slot_in, b_in, b_slot_in, mask_in, out,
    a_slot, b_slot, mask, a_buf, b_buf, a_tab, b_tab, tab_v, tab_s, sel, tx, tx_scale, rx, rx_scale, comp,
    in_sem, own_sem, z_in, x_in, y_in, sib_in, a_recv, b_recv, sib_recv, tab_recv, tab_local,
    a_send, b_send, tab_send, rs_recv, rs_send,
):
    x, z, layer = lax.axis_index("row"), lax.axis_index("col"), lax.axis_index("layer")
    y, core = lax.div(layer, 2), lax.rem(layer, 2)
    other = 1 - core
    twin = y * 2 + other
    sibling = {"layer": twin}
    y_up, y_down = lax.rem(y + 1, RING), lax.rem(y + RING - 1, RING)
    loads = [
        pltpu.make_async_copy(a_slot_in, a_slot, in_sem.at[0]),
        pltpu.make_async_copy(b_slot_in, b_slot, in_sem.at[1]),
        pltpu.make_async_copy(mask_in, mask, in_sem.at[2]),
    ]
    for copy in loads:
        copy.start()

    barrier = pltpu.get_barrier_semaphore()

    def flag(condition):
        return jnp.where(condition, 1, 0)

    def signal(sem, device):
        pl.semaphore_signal(sem, inc=1, device_id=device, device_id_type=MESH)

    at_x, at_y, at_z, at_core = flag(x == 0), flag(y == 0), flag(z == 0), flag(core == 0)
    is_zero = at_x * at_y * at_z * at_core
    x_place, y_place = place(x, X_ORDER), place(y, Y_ORDER)
    z_rank, x_rank, y_rank = z + 8 * is_zero, x_place + 8 * is_zero, y_place + 8 * is_zero
    core_rank = core + 2 * is_zero
    sib_rank = other + 2 * (at_x * at_y * at_z * core)

    def z_peer(p, twin):
        return p + (8 * (at_x * at_y * (core if twin else at_core)) if p == 0 else 0)

    def x_peer(p, twin):
        return X_ORDER.index(p) + (8 * (at_y * at_z * (core if twin else at_core)) if p == 0 else 0)

    def y_peer(p):
        return place(p, Y_ORDER) + 8 * (at_x * at_z * core * flag(p == 0))

    def after(peer, me, fn, *args):
        pl.when(peer > me)(functools.partial(fn, *args))

    def before(peer, me, fn, *args):
        pl.when(peer < me)(functools.partial(fn, *args))

    def ring(place, own_zero, twin_zero):
        spot = lax.rem(place - own_zero + RING, RING)
        turn = twin_zero * flag(place > 0)
        twin_spot = place - turn

        def over(first, end, shift, fn):
            def step(n, carry):
                fn(lax.rem(n + shift, RING))
                return carry

            lax.fori_loop(first, end, step, 0)

        def all_before(fn):
            over(0, spot, own_zero, fn)

        def all_after(fn):
            over(spot + 1, RING, own_zero, fn)

        def twins_before(fn):
            over(is_zero, twin_spot + 8 * is_zero, turn, fn)

        def twins_after(fn):
            over(twin_spot + 1 + 8 * is_zero, RING, turn, fn)

        return all_before, all_after, twins_before, twins_after

    z_before, z_later, z_twins_before, z_twins_later = ring(z, at_x * at_y * at_core, at_x * at_y * core)
    x_before, x_later, x_twins_before, x_twins_later = ring(x_place, at_y * at_z * at_core, at_y * at_z * core)

    def col(p):
        return {"col": p}

    def col_twin(p):
        return {"col": p, "layer": twin}

    def row(n):
        return {"row": member(n, X_ORDER)}

    def row_twin(n):
        return {"row": member(n, X_ORDER), "layer": twin}

    after(sib_rank, core_rank, signal, barrier, sibling)
    for peer in (y_up, y_down):
        after(y_peer(peer), y_rank, signal, barrier, {"layer": peer * 2 + other})
    x_later(lambda n: signal(barrier, row(n)))
    x_twins_later(lambda n: signal(barrier, row_twin(n)))
    z_later(lambda p: signal(barrier, col(p)))
    z_twins_later(lambda p: signal(barrier, col_twin(p)))

    own_a = core * 16 + z * 2
    own_b = core * 8 + x
    own = [
        pltpu.make_async_copy(a_in, a_buf.at[pl.ds(own_a, 2)], own_sem.at[0]),
        pltpu.make_async_copy(b_in, b_buf.at[pl.ds(own_b, 1)], own_sem.at[1]),
    ]
    for copy in own:
        copy.start()
    z_lower = 2 * z - flag(z > 0) * at_x * at_y
    x_lower = 2 * x_place - flag(x > 0) * at_y * at_z
    y_lower = flag(y_peer(y_up) < y_rank) + flag(y_peer(y_down) < y_rank)
    n_lower = jnp.where(is_zero == 1, 4 * (RING - 1), z_lower + x_lower) + y_lower + flag(sib_rank < core_rank)

    @pl.when(n_lower > 0)
    def _():
        pl.semaphore_wait(barrier, n_lower)

    def push(src, dst, send, recv, device):
        pltpu.make_async_remote_copy(
            src_ref=src, dst_ref=dst, send_sem=send, recv_sem=recv, device_id=device, device_id_type=MESH
        ).start()

    def push_a(p):
        push(a_in, a_buf.at[pl.ds(own_a, 2)], a_send, a_recv.at[z], col(p))

    def push_b(device):
        push(b_in, b_buf.at[pl.ds(own_b, 1)], b_send, b_recv.at[x], device)

    def push_a_tab(device):
        row = a_tab.at[core * 8 + z]
        push(row, row, tab_send.at[0], tab_recv.at[0], device)

    def push_b_tab(device):
        row = b_tab.at[core * 8 + x]
        push(row, row, tab_send.at[1], tab_recv.at[1], device)

    group = lax.div(z, 4)
    is_end = flag(z == 0) + flag(z == 3) + flag(z == 4) + flag(z == 7)
    line_of_zero = at_x * at_y * at_core
    z_inner = {"col": z + 1 - 2 * lax.rem(z, 2)}

    def any_of(index, planes):
        return sum((flag(index == p) for p in planes), jnp.int32(0))

    def push_a_if_direct(p):
        near = flag(lax.div(p, 4) == group)
        end = flag(p == 0) + flag(p == 3) + flag(p == 4) + flag(p == 7)
        extra = flag(p == 1) * any_of(z, DIRECT_TO_1) + flag(p == 2) * any_of(z, DIRECT_TO_2)
        pl.when(near + end + extra > 0)(functools.partial(push_a, p))

    z_before(push_a_if_direct)

    for copy in loads[:2]:
        copy.wait()
    lane = lax.broadcasted_iota(jnp.int32, (1, BS), 1)
    first = jnp.where(lane == core * 64 + a_slot[0], own_a + 1, 0)
    a_tab[core * 8 + z] = jnp.where(lane == core * 64 + a_slot[1], own_a + 2, first)
    b_tab[core * 8 + x] = jnp.where(lane == core * 32 + b_slot[0], own_b + 1, 0)

    z_before(lambda p: push_a_tab(col(p)))
    z_twins_before(lambda p: push_a_tab(col_twin(p)))
    z_before(lambda p: signal(z_in.at[core, z], col(p)))
    z_twins_before(lambda p: signal(z_in.at[core, z], col_twin(p)))
    x_before(lambda n: push_b(row(n)))
    x_before(lambda n: push_b_tab(row(n)))
    x_twins_before(lambda n: push_b_tab(row_twin(n)))
    x_before(lambda n: signal(x_in.at[core, x], row(n)))
    x_twins_before(lambda n: signal(x_in.at[core, x], row_twin(n)))

    before(y_peer(y_up), y_rank, signal, y_in.at[1], {"layer": y_up * 2 + other})
    before(y_peer(y_down), y_rank, signal, y_in.at[0], {"layer": y_down * 2 + other})
    before(sib_rank, core_rank, signal, sib_in, sibling)

    @pl.when(sib_rank > core_rank)
    def _():
        pl.semaphore_wait(sib_in, 1)

    push(a_in, a_buf.at[pl.ds(own_a, 2)], a_send, sib_recv.at[0], sibling)
    push(b_in, b_buf.at[pl.ds(own_b, 1)], b_send, sib_recv.at[1], sibling)
    push_a_tab(sibling)
    push_b_tab(sibling)

    a_buf[32] = jnp.zeros((BS, BS), jnp.bfloat16)
    b_buf[16] = jnp.zeros((BS, BS), jnp.bfloat16)
    comp[KEPT] = jnp.zeros((BS, BS), jnp.float32)

    def x_after(p):
        pl.semaphore_wait(x_in.at[core, p], 1)
        push_b({"row": p})
        push_b_tab({"row": p})

    def x_after_twin(p):
        pl.semaphore_wait(x_in.at[other, p], 1)
        push_b_tab({"row": p, "layer": twin})

    for p in X_ORDER[1:] + (0,):

        @pl.when(p != x)
        def _():
            after(x_peer(p, 0), x_rank, x_after, p)
            after(x_peer(p, 1), x_rank, x_after_twin, p)

    loads[2].wait()

    def pick(t, carry):
        count = jnp.int32(0)
        picks = [jnp.int32(0)] * KEPT
        for j in range(COLS):
            bit = mask[j, t]
            for q in range(KEPT):
                picks[q] = picks[q] + jnp.where(count == q, bit * j, 0)
            count = count + bit
        for q in range(KEPT):
            sel[t, q] = picks[q]
        return carry

    lax.fori_loop(0, ROWS, pick, 0)

    def z_after(p):
        pl.semaphore_wait(z_in.at[core, p], 1)
        push_a_if_direct(p)
        push_a_tab({"col": p})

    def z_after_twin(p):
        pl.semaphore_wait(z_in.at[other, p], 1)
        push_a_tab({"col": p, "layer": twin})

    def offer(peers):
        for p in peers:

            @pl.when(p != z)
            def _():
                after(z_peer(p, 0), z_rank, z_after, p)
                after(z_peer(p, 1), z_rank, z_after_twin, p)

    def share_b():
        for p in range(RING):

            @pl.when(p != x)
            def _():
                block = b_buf.at[pl.ds(core * 8 + p, 1)]
                wait_bytes(block, b_recv.at[p])
                push(block, block, b_send, sib_recv.at[1], sibling)

    def share_a(peers):
        for p in peers:

            @pl.when(p != z)
            def _():
                blocks = a_buf.at[pl.ds(core * 16 + p * 2, 2)]
                wait_bytes(blocks, a_recv.at[p])

                inwards = is_end * flag(group != p // 4)
                if p in DIRECT_TO_1:
                    inwards = inwards * flag(z != 0)
                if p in DIRECT_TO_2:
                    inwards = inwards * flag(z != 3)

                @pl.when(inwards == 1)
                def _():
                    push(blocks, blocks, a_send, a_recv.at[p], z_inner)

                push(blocks, blocks, a_send, sib_recv.at[0], sibling)

    forwards = (flag(z == 0) + flag(z == 3)) * (1 - line_of_zero)
    offer((1, 2, 3))

    @pl.when(group == 0)
    def _():
        share_b()
        share_a((1, 2, 3))

    offer((4, 5))

    @pl.when(forwards == 1)
    def _():
        share_a((4,))

    offer((6,))

    @pl.when(forwards == 1)
    def _():
        share_a((5,))

    offer((7, 0))

    @pl.when(y_peer(y_up) > y_rank)
    def _():
        pl.semaphore_wait(y_in.at[0], 1)

    @pl.when(y_peer(y_down) > y_rank)
    def _():
        pl.semaphore_wait(y_in.at[1], 1)

    @pl.when(group == 1)
    def _():
        share_b()
        share_a((1, 2, 3))

    @pl.when(forwards == 0)
    def _():
        share_a((4, 5))

    share_a((6, 7, 0))
    wait_bytes(a_tab.at[pl.ds(0, 15)], tab_recv.at[0])
    wait_bytes(b_tab.at[pl.ds(0, 15)], tab_recv.at[1])
    a_at, b_at = jnp.max(a_tab[...], axis=0), jnp.max(b_tab[...], axis=0)
    tab_v[0] = jnp.where(a_at > 0, a_at - 1, 32)
    tab_v[1] = jnp.where(b_at > 0, b_at - 1, 16)
    to_scalars = pltpu.make_async_copy(tab_v, tab_s, tab_local)
    to_scalars.start()
    for copy in own:
        copy.wait()
    to_scalars.wait()
    wait_bytes(a_buf.at[pl.ds(other * 16, 16)], sib_recv.at[0])
    wait_bytes(b_buf.at[pl.ds(other * 8, 8)], sib_recv.at[1])

    slices = [(s, kk) for s in range(2) for kk in range(INNER)]

    def partial(row):
        left = jnp.concatenate([a_buf[tab_s[0, 0, s * 64 + row * INNER + kk]] for s, kk in slices], axis=1)
        sums = []
        for p in range(KEPT // 2):
            right = jnp.concatenate(
                [
                    jnp.concatenate(
                        [b_buf[tab_s[1, 0, s * 32 + kk * COLS + sel[row, 2 * p + q]]] for q in range(2)], axis=1
                    )
                    for s, kk in slices
                ],
                axis=0,
            )
            both = jnp.dot(left, right, preferred_element_type=jnp.float32)
            sums += [both[:, :BS], both[:, BS:]]
        return sums

    def received(slot, q):
        wait_bytes(rx_scale.at[slot, q], rs_recv.at[slot, q, 1])
        wait_bytes(rx.at[slot, q], rs_recv.at[slot, q, 0])
        return rx[slot, q].astype(jnp.int32).astype(jnp.float32) * rx_scale[slot, q]

    def send(slot, q, value, device):
        top = jnp.maximum(jnp.max(jnp.abs(value), axis=0, keepdims=True), TINY)
        tx_scale[slot, q] = top * (1.0 / TOP)
        tx[slot, q] = jnp.round(value * (TOP / top)).astype(jnp.int32).astype(jnp.int16)
        push(tx_scale.at[slot, q], rx_scale.at[slot, q], rs_send.at[1], rs_recv.at[slot, q, 1], device)
        push(tx.at[slot, q], rx.at[slot, q], rs_send.at[0], rs_recv.at[slot, q, 0], device)

    to_up, to_down = {"layer": y_up * 2 + other}, {"layer": y_down * 2 + other}
    up_half, down_half = (0, 1), (2, 3)
    sums = partial(lax.rem(y + 4, RING) * 2 + core)
    for q in up_half:
        send(0, q, sums[q], to_up)
    for q in down_half:
        send(4, q, sums[q], to_down)
    for hop in range(1, 4):
        turned = other if hop % 2 else core
        up = partial(lax.rem(y + 4 - hop, RING) * 2 + turned)
        down = partial(lax.rem(y + 4 + hop, RING) * 2 + turned)
        for q in down_half:
            send(hop, q, up[q] if hop == 1 else up[q] + received(hop - 1, q), to_up)
        for q in up_half:
            send(4 + hop, q, down[q] if hop == 1 else down[q] + received(3 + hop, q), to_down)
        for q in up_half:
            send(hop, q, up[q] + received(hop - 1, q), to_up)
        for q in down_half:
            send(4 + hop, q, down[q] + received(3 + hop, q), to_down)
    sums = partial(layer)
    for q in down_half + up_half:
        comp[q] = sums[q] + received(3, q) + received(7, q)
    count = jnp.int32(0)
    for j in range(COLS):
        bit = mask[j, layer]
        out[:, j * BS : (j + 1) * BS] = comp[jnp.where(bit == 1, count, KEPT)]
        count = count + bit

    wait_bytes(a_buf.at[pl.ds(0, 26)], a_send)
    for plane, more in (
        (0, 4 - len(DIRECT_TO_1)),
        (3, 4 - len(DIRECT_TO_2)),
        (4, 4 + (4 in DIRECT_TO_1) + (4 in DIRECT_TO_2)),
        (5, (5 in DIRECT_TO_1) + (5 in DIRECT_TO_2)),
        (6, (6 in DIRECT_TO_1) + (6 in DIRECT_TO_2)),
        (7, 4 + (7 in DIRECT_TO_1) + (7 in DIRECT_TO_2)),
    ):
        if more:

            @pl.when(z == plane)
            def _():
                wait_bytes(a_buf.at[pl.ds(0, 2 * more)], a_send)

    wait_bytes(b_buf.at[pl.ds(0, 15)], b_send)
    wait_bytes(a_tab.at[pl.ds(0, 15)], tab_send.at[0])
    wait_bytes(b_tab.at[pl.ds(0, 15)], tab_send.at[1])
    wait_bytes(tx.at[pl.ds(0, 7)], rs_send.at[0])
    wait_bytes(tx_scale.at[pl.ds(0, 7)], rs_send.at[1])


def on_device(a_blocks, a_slot, b_blocks, b_slot, c_mask):
    vmem, smem, dma = pltpu.VMEM, pltpu.SMEM, pltpu.SemaphoreType.DMA
    regular = pltpu.SemaphoreType.REGULAR
    operands = (a_blocks, a_slot, b_blocks, b_slot, c_mask.T)
    operands = [operand if operand is b_slot else pltpu.with_memory_space_constraint(operand, pltpu.HBM) for operand in operands]
    return pl.pallas_call(
        kernel,
        out_shape=jax.ShapeDtypeStruct((BS, COLS * BS), jnp.float32),
        in_specs=[pl.BlockSpec(memory_space=pltpu.HBM)] * 5,
        out_specs=pl.BlockSpec(memory_space=vmem),
        scratch_shapes=[
            smem((2,), jnp.int32),
            smem((1,), jnp.int32),
            smem((COLS, ROWS), jnp.int32),
            vmem((33, BS, BS), jnp.bfloat16),
            vmem((17, BS, BS), jnp.bfloat16),
            vmem((2 * RING, 1, BS), jnp.int32),
            vmem((2 * RING, 1, BS), jnp.int32),
            vmem((2, 1, BS), jnp.int32),
            smem((2, 1, BS), jnp.int32),
            smem((ROWS, KEPT), jnp.int32),
            vmem((8, KEPT, BS, BS), jnp.int16),
            vmem((8, KEPT, 1, BS), jnp.float32),
            vmem((8, KEPT, BS, BS), jnp.int16),
            vmem((8, KEPT, 1, BS), jnp.float32),
            vmem((KEPT + 1, BS, BS), jnp.float32),
            dma((3,)),
            dma((2,)),
            regular((2, RING)),
            regular((2, RING)),
            regular((2,)),
            regular(()),
            dma((RING,)),
            dma((RING,)),
            dma((2,)),
            dma((2,)),
            dma(()),
            dma(()),
            dma(()),
            dma((2,)),
            dma((8, KEPT, 2)),
            dma((2,)),
        ],
        compiler_params=pltpu.CompilerParams(
            collective_id=0, has_side_effects=True, vmem_limit_bytes=40 * 1024 * 1024
        ),
    )(*operands)


def solution(mesh):
    in_specs = (
        P(("row", "col", "layer"), None, None),
        P(("row", "col", "layer")),
        P(("row", "col", "layer"), None, None),
        P(("row", "col", "layer")),
        P("row", "col"),
    )
    out_specs = P(("row", "layer"), "col")
    return jax.shard_map(on_device, mesh=mesh, in_specs=in_specs, out_specs=out_specs, check_vma=False)
```

```python
import functools

import jax
import jax.numpy as jnp
from jax import lax
from jax.experimental import pallas as pl
from jax.experimental.pallas import tpu as pltpu
from jax.sharding import PartitionSpec as P

MESH = pl.DeviceIdType.MESH
BS = 128
ROWS = 16
INNER = 4
COLS = 8
KEPT = 4
RING = 8
TOP = 32760.0
TINY = 1e-30


DIRECT_TO_1, DIRECT_TO_2 = (6, 7), ()
X_ORDER = Y_ORDER = (0, 1, 2, 3, 7, 6, 5, 4)


def place(index, order):
    found = jnp.int32(0)
    for n, p in enumerate(order):
        found = jnp.where(index == p, n, found)
    return found


def member(n, order):
    found = jnp.int32(0)
    for m, p in enumerate(order):
        found = jnp.where(n == m, p, found)
    return found


def wait_bytes(ref, sem):
    pltpu.make_async_copy(ref, ref, sem).wait()


def kernel(
    a_in, a_slot_in, b_in, b_slot_in, mask_in, out,
    a_slot, b_slot, mask, a_buf, b_buf, a_tab, b_tab, tab_v, tab_s, sel, tx, tx_scale, rx, rx_scale, comp,
    in_sem, own_sem, z_in, x_in, y_in, sib_in, a_recv, b_recv, sib_recv, tab_recv, tab_local,
    a_send, b_send, tab_send, rs_recv, rs_send,
):
    x, z, layer = lax.axis_index("row"), lax.axis_index("col"), lax.axis_index("layer")
    y, core = lax.div(layer, 2), lax.rem(layer, 2)
    other = 1 - core
    twin = y * 2 + other
    sibling = {"layer": twin}
    y_up, y_down = lax.rem(y + 1, RING), lax.rem(y + RING - 1, RING)
    loads = [
        pltpu.make_async_copy(a_slot_in, a_slot, in_sem.at[0]),
        pltpu.make_async_copy(b_slot_in, b_slot, in_sem.at[1]),
        pltpu.make_async_copy(mask_in, mask, in_sem.at[2]),
    ]
    for copy in loads:
        copy.start()

    barrier = pltpu.get_barrier_semaphore()

    def flag(condition):
        return jnp.where(condition, 1, 0)

    def signal(sem, device):
        pl.semaphore_signal(sem, inc=1, device_id=device, device_id_type=MESH)

    at_x, at_y, at_z, at_core = flag(x == 0), flag(y == 0), flag(z == 0), flag(core == 0)
    is_zero = at_x * at_y * at_z * at_core
    x_place, y_place = place(x, X_ORDER), place(y, Y_ORDER)
    z_rank, x_rank, y_rank = z + 8 * is_zero, x_place + 8 * is_zero, y_place + 8 * is_zero
    core_rank = core + 2 * is_zero
    sib_rank = other + 2 * (at_x * at_y * at_z * core)

    def z_peer(p, twin):
        return p + (8 * (at_x * at_y * (core if twin else at_core)) if p == 0 else 0)

    def x_peer(p, twin):
        return X_ORDER.index(p) + (8 * (at_y * at_z * (core if twin else at_core)) if p == 0 else 0)

    def y_peer(p):
        return place(p, Y_ORDER) + 8 * (at_x * at_z * core * flag(p == 0))

    def after(peer, me, fn, *args):
        pl.when(peer > me)(functools.partial(fn, *args))

    def before(peer, me, fn, *args):
        pl.when(peer < me)(functools.partial(fn, *args))

    def ring(place, own_zero, twin_zero):
        spot = lax.rem(place - own_zero + RING, RING)
        turn = twin_zero * flag(place > 0)
        twin_spot = place - turn

        def over(first, end, shift, fn):
            def step(n, carry):
                fn(lax.rem(n + shift, RING))
                return carry

            lax.fori_loop(first, end, step, 0)

        def all_before(fn):
            over(0, spot, own_zero, fn)

        def all_after(fn):
            over(spot + 1, RING, own_zero, fn)

        def twins_before(fn):
            over(is_zero, twin_spot + 8 * is_zero, turn, fn)

        def twins_after(fn):
            over(twin_spot + 1 + 8 * is_zero, RING, turn, fn)

        return all_before, all_after, twins_before, twins_after

    z_before, z_later, z_twins_before, z_twins_later = ring(z, at_x * at_y * at_core, at_x * at_y * core)
    x_before, x_later, x_twins_before, x_twins_later = ring(x_place, at_y * at_z * at_core, at_y * at_z * core)

    def col(p):
        return {"col": p}

    def col_twin(p):
        return {"col": p, "layer": twin}

    def row(n):
        return {"row": member(n, X_ORDER)}

    def row_twin(n):
        return {"row": member(n, X_ORDER), "layer": twin}

    after(sib_rank, core_rank, signal, barrier, sibling)
    for peer in (y_up, y_down):
        after(y_peer(peer), y_rank, signal, barrier, {"layer": peer * 2 + other})
    x_later(lambda n: signal(barrier, row(n)))
    x_twins_later(lambda n: signal(barrier, row_twin(n)))
    z_later(lambda p: signal(barrier, col(p)))
    z_twins_later(lambda p: signal(barrier, col_twin(p)))

    own_a = core * 16 + z * 2
    own_b = core * 8 + x
    own = [
        pltpu.make_async_copy(a_in, a_buf.at[pl.ds(own_a, 2)], own_sem.at[0]),
        pltpu.make_async_copy(b_in, b_buf.at[pl.ds(own_b, 1)], own_sem.at[1]),
    ]
    for copy in own:
        copy.start()
    z_lower = 2 * z - flag(z > 0) * at_x * at_y
    x_lower = 2 * x_place - flag(x > 0) * at_y * at_z
    y_lower = flag(y_peer(y_up) < y_rank) + flag(y_peer(y_down) < y_rank)
    n_lower = jnp.where(is_zero == 1, 4 * (RING - 1), z_lower + x_lower) + y_lower + flag(sib_rank < core_rank)

    @pl.when(n_lower > 0)
    def _():
        pl.semaphore_wait(barrier, n_lower)

    def push(src, dst, send, recv, device):
        pltpu.make_async_remote_copy(
            src_ref=src, dst_ref=dst, send_sem=send, recv_sem=recv, device_id=device, device_id_type=MESH
        ).start()

    def push_a(p):
        push(a_in, a_buf.at[pl.ds(own_a, 2)], a_send, a_recv.at[z], col(p))

    def push_b(device):
        push(b_in, b_buf.at[pl.ds(own_b, 1)], b_send, b_recv.at[x], device)

    def push_a_tab(device):
        row = a_tab.at[core * 8 + z]
        push(row, row, tab_send.at[0], tab_recv.at[0], device)

    def push_b_tab(device):
        row = b_tab.at[core * 8 + x]
        push(row, row, tab_send.at[1], tab_recv.at[1], device)

    group = lax.div(z, 4)
    is_end = flag(z == 0) + flag(z == 3) + flag(z == 4) + flag(z == 7)
    line_of_zero = at_x * at_y * at_core
    z_inner = {"col": z + 1 - 2 * lax.rem(z, 2)}

    def any_of(index, planes):
        return sum((flag(index == p) for p in planes), jnp.int32(0))

    def push_a_if_direct(p):
        near = flag(lax.div(p, 4) == group)
        end = flag(p == 0) + flag(p == 3) + flag(p == 4) + flag(p == 7)
        extra = flag(p == 1) * any_of(z, DIRECT_TO_1) + flag(p == 2) * any_of(z, DIRECT_TO_2)
        pl.when(near + end + extra > 0)(functools.partial(push_a, p))

    def announce_z():
        z_before(lambda p: signal(z_in.at[core, z], col(p)))
        z_twins_before(lambda p: signal(z_in.at[core, z], col_twin(p)))

    def announce_x():
        x_before(lambda n: signal(x_in.at[core, x], row(n)))
        x_twins_before(lambda n: signal(x_in.at[core, x], row_twin(n)))

    @pl.when(is_zero == 1)
    def _():
        announce_z()
        announce_x()

    z_before(push_a_if_direct)

    for copy in loads[:2]:
        copy.wait()
    lane = lax.broadcasted_iota(jnp.int32, (1, BS), 1)
    first = jnp.where(lane == core * 64 + a_slot[0], own_a + 1, 0)
    a_tab[core * 8 + z] = jnp.where(lane == core * 64 + a_slot[1], own_a + 2, first)
    b_tab[core * 8 + x] = jnp.where(lane == core * 32 + b_slot[0], own_b + 1, 0)

    z_before(lambda p: push_a_tab(col(p)))
    z_twins_before(lambda p: push_a_tab(col_twin(p)))
    pl.when(is_zero == 0)(announce_z)
    x_before(lambda n: push_b(row(n)))
    x_before(lambda n: push_b_tab(row(n)))
    x_twins_before(lambda n: push_b_tab(row_twin(n)))
    pl.when(is_zero == 0)(announce_x)

    before(y_peer(y_up), y_rank, signal, y_in.at[1], {"layer": y_up * 2 + other})
    before(y_peer(y_down), y_rank, signal, y_in.at[0], {"layer": y_down * 2 + other})
    before(sib_rank, core_rank, signal, sib_in, sibling)

    @pl.when(sib_rank > core_rank)
    def _():
        pl.semaphore_wait(sib_in, 1)

    push(a_in, a_buf.at[pl.ds(own_a, 2)], a_send, sib_recv.at[0], sibling)
    push(b_in, b_buf.at[pl.ds(own_b, 1)], b_send, sib_recv.at[1], sibling)
    push_a_tab(sibling)
    push_b_tab(sibling)

    a_buf[32] = jnp.zeros((BS, BS), jnp.bfloat16)
    b_buf[16] = jnp.zeros((BS, BS), jnp.bfloat16)
    comp[KEPT] = jnp.zeros((BS, BS), jnp.float32)

    def x_after(p):
        pl.semaphore_wait(x_in.at[core, p], 1)
        push_b({"row": p})
        push_b_tab({"row": p})

    def x_after_twin(p):
        pl.semaphore_wait(x_in.at[other, p], 1)
        push_b_tab({"row": p, "layer": twin})

    for p in X_ORDER[1:] + (0,):

        @pl.when(p != x)
        def _():
            after(x_peer(p, 0), x_rank, x_after, p)
            after(x_peer(p, 1), x_rank, x_after_twin, p)

    loads[2].wait()

    def pick(t, carry):
        count = jnp.int32(0)
        picks = [jnp.int32(0)] * KEPT
        for j in range(COLS):
            bit = mask[j, t]
            for q in range(KEPT):
                picks[q] = picks[q] + jnp.where(count == q, bit * j, 0)
            count = count + bit
        for q in range(KEPT):
            sel[t, q] = picks[q]
        return carry

    lax.fori_loop(0, ROWS, pick, 0)

    def z_after(p):
        pl.semaphore_wait(z_in.at[core, p], 1)
        push_a_if_direct(p)
        push_a_tab({"col": p})

    def z_after_twin(p):
        pl.semaphore_wait(z_in.at[other, p], 1)
        push_a_tab({"col": p, "layer": twin})

    def offer(peers):
        for p in peers:

            @pl.when(p != z)
            def _():
                after(z_peer(p, 0), z_rank, z_after, p)
                after(z_peer(p, 1), z_rank, z_after_twin, p)

    def share_b():
        for p in range(RING):

            @pl.when(p != x)
            def _():
                block = b_buf.at[pl.ds(core * 8 + p, 1)]
                wait_bytes(block, b_recv.at[p])
                push(block, block, b_send, sib_recv.at[1], sibling)

    def share_a(peers):
        for p in peers:

            @pl.when(p != z)
            def _():
                blocks = a_buf.at[pl.ds(core * 16 + p * 2, 2)]
                wait_bytes(blocks, a_recv.at[p])

                inwards = is_end * flag(group != p // 4)
                if p in DIRECT_TO_1:
                    inwards = inwards * flag(z != 0)
                if p in DIRECT_TO_2:
                    inwards = inwards * flag(z != 3)

                @pl.when(inwards == 1)
                def _():
                    push(blocks, blocks, a_send, a_recv.at[p], z_inner)

                push(blocks, blocks, a_send, sib_recv.at[0], sibling)

    forwards = (flag(z == 0) + flag(z == 3)) * (1 - line_of_zero)
    offer((1, 2, 3))

    @pl.when(group == 0)
    def _():
        share_b()
        share_a((1, 2, 3))

    offer((4, 5))

    @pl.when(forwards == 1)
    def _():
        share_a((4,))

    offer((6,))

    @pl.when(forwards == 1)
    def _():
        share_a((5,))

    offer((7, 0))

    @pl.when(y_peer(y_up) > y_rank)
    def _():
        pl.semaphore_wait(y_in.at[0], 1)

    @pl.when(y_peer(y_down) > y_rank)
    def _():
        pl.semaphore_wait(y_in.at[1], 1)

    @pl.when(group == 1)
    def _():
        share_b()
        share_a((1, 2, 3))

    @pl.when(forwards == 0)
    def _():
        share_a((4, 5))

    share_a((6, 7, 0))
    wait_bytes(a_tab.at[pl.ds(0, 15)], tab_recv.at[0])
    wait_bytes(b_tab.at[pl.ds(0, 15)], tab_recv.at[1])
    a_at, b_at = jnp.max(a_tab[...], axis=0), jnp.max(b_tab[...], axis=0)
    tab_v[0] = jnp.where(a_at > 0, a_at - 1, 32)
    tab_v[1] = jnp.where(b_at > 0, b_at - 1, 16)
    to_scalars = pltpu.make_async_copy(tab_v, tab_s, tab_local)
    to_scalars.start()
    for copy in own:
        copy.wait()
    to_scalars.wait()
    wait_bytes(a_buf.at[pl.ds(other * 16, 16)], sib_recv.at[0])
    wait_bytes(b_buf.at[pl.ds(other * 8, 8)], sib_recv.at[1])

    slices = [(s, kk) for s in range(2) for kk in range(INNER)]

    def partial(row):
        left = jnp.concatenate([a_buf[tab_s[0, 0, s * 64 + row * INNER + kk]] for s, kk in slices], axis=1)
        sums = []
        for p in range(KEPT // 2):
            right = jnp.concatenate(
                [
                    jnp.concatenate(
                        [b_buf[tab_s[1, 0, s * 32 + kk * COLS + sel[row, 2 * p + q]]] for q in range(2)], axis=1
                    )
                    for s, kk in slices
                ],
                axis=0,
            )
            both = jnp.dot(left, right, preferred_element_type=jnp.float32)
            sums += [both[:, :BS], both[:, BS:]]
        return sums

    def received(slot, q):
        wait_bytes(rx_scale.at[slot, q], rs_recv.at[slot, q, 1])
        wait_bytes(rx.at[slot, q], rs_recv.at[slot, q, 0])
        return rx[slot, q].astype(jnp.int32).astype(jnp.float32) * rx_scale[slot, q]

    def send(slot, q, value, device):
        top = jnp.maximum(jnp.max(jnp.abs(value), axis=0, keepdims=True), TINY)
        tx_scale[slot, q] = top * (1.0 / TOP)
        tx[slot, q] = jnp.round(value * (TOP / top)).astype(jnp.int32).astype(jnp.int16)
        push(tx_scale.at[slot, q], rx_scale.at[slot, q], rs_send.at[1], rs_recv.at[slot, q, 1], device)
        push(tx.at[slot, q], rx.at[slot, q], rs_send.at[0], rs_recv.at[slot, q, 0], device)

    to_up, to_down = {"layer": y_up * 2 + other}, {"layer": y_down * 2 + other}
    up_half, down_half = (0, 1), (2, 3)
    sums = partial(lax.rem(y + 4, RING) * 2 + core)
    for q in up_half:
        send(0, q, sums[q], to_up)
    for q in down_half:
        send(4, q, sums[q], to_down)
    for hop in range(1, 4):
        turned = other if hop % 2 else core
        up = partial(lax.rem(y + 4 - hop, RING) * 2 + turned)
        down = partial(lax.rem(y + 4 + hop, RING) * 2 + turned)
        for q in down_half:
            send(hop, q, up[q] if hop == 1 else up[q] + received(hop - 1, q), to_up)
        for q in up_half:
            send(4 + hop, q, down[q] if hop == 1 else down[q] + received(3 + hop, q), to_down)
        for q in up_half:
            send(hop, q, up[q] + received(hop - 1, q), to_up)
        for q in down_half:
            send(4 + hop, q, down[q] + received(3 + hop, q), to_down)
    sums = partial(layer)
    for q in down_half + up_half:
        comp[q] = sums[q] + received(3, q) + received(7, q)
    count = jnp.int32(0)
    for j in range(COLS):
        bit = mask[j, layer]
        out[:, j * BS : (j + 1) * BS] = comp[jnp.where(bit == 1, count, KEPT)]
        count = count + bit

    wait_bytes(a_buf.at[pl.ds(0, 26)], a_send)
    for plane, more in (
        (0, 4 - len(DIRECT_TO_1)),
        (3, 4 - len(DIRECT_TO_2)),
        (4, 4 + (4 in DIRECT_TO_1) + (4 in DIRECT_TO_2)),
        (5, (5 in DIRECT_TO_1) + (5 in DIRECT_TO_2)),
        (6, (6 in DIRECT_TO_1) + (6 in DIRECT_TO_2)),
        (7, 4 + (7 in DIRECT_TO_1) + (7 in DIRECT_TO_2)),
    ):
        if more:

            @pl.when(z == plane)
            def _():
                wait_bytes(a_buf.at[pl.ds(0, 2 * more)], a_send)

    wait_bytes(b_buf.at[pl.ds(0, 15)], b_send)
    wait_bytes(a_tab.at[pl.ds(0, 15)], tab_send.at[0])
    wait_bytes(b_tab.at[pl.ds(0, 15)], tab_send.at[1])
    wait_bytes(tx.at[pl.ds(0, 7)], rs_send.at[0])
    wait_bytes(tx_scale.at[pl.ds(0, 7)], rs_send.at[1])


def on_device(a_blocks, a_slot, b_blocks, b_slot, c_mask):
    vmem, smem, dma = pltpu.VMEM, pltpu.SMEM, pltpu.SemaphoreType.DMA
    regular = pltpu.SemaphoreType.REGULAR
    operands = (a_blocks, a_slot, b_blocks, b_slot, c_mask.T)
    operands = [operand if operand is b_slot else pltpu.with_memory_space_constraint(operand, pltpu.HBM) for operand in operands]
    return pl.pallas_call(
        kernel,
        out_shape=jax.ShapeDtypeStruct((BS, COLS * BS), jnp.float32),
        in_specs=[pl.BlockSpec(memory_space=pltpu.HBM)] * 5,
        out_specs=pl.BlockSpec(memory_space=vmem),
        scratch_shapes=[
            smem((2,), jnp.int32),
            smem((1,), jnp.int32),
            smem((COLS, ROWS), jnp.int32),
            vmem((33, BS, BS), jnp.bfloat16),
            vmem((17, BS, BS), jnp.bfloat16),
            vmem((2 * RING, 1, BS), jnp.int32),
            vmem((2 * RING, 1, BS), jnp.int32),
            vmem((2, 1, BS), jnp.int32),
            smem((2, 1, BS), jnp.int32),
            smem((ROWS, KEPT), jnp.int32),
            vmem((8, KEPT, BS, BS), jnp.int16),
            vmem((8, KEPT, 1, BS), jnp.float32),
            vmem((8, KEPT, BS, BS), jnp.int16),
            vmem((8, KEPT, 1, BS), jnp.float32),
            vmem((KEPT + 1, BS, BS), jnp.float32),
            dma((3,)),
            dma((2,)),
            regular((2, RING)),
            regular((2, RING)),
            regular((2,)),
            regular(()),
            dma((RING,)),
            dma((RING,)),
            dma((2,)),
            dma((2,)),
            dma(()),
            dma(()),
            dma(()),
            dma((2,)),
            dma((8, KEPT, 2)),
            dma((2,)),
        ],
        compiler_params=pltpu.CompilerParams(
            collective_id=0, has_side_effects=True, vmem_limit_bytes=40 * 1024 * 1024
        ),
    )(*operands)


def solution(mesh):
    in_specs = (
        P(("row", "col", "layer"), None, None),
        P(("row", "col", "layer")),
        P(("row", "col", "layer"), None, None),
        P(("row", "col", "layer")),
        P("row", "col"),
    )
    out_specs = P(("row", "layer"), "col")
    return jax.shard_map(on_device, mesh=mesh, in_specs=in_specs, out_specs=out_specs, check_vma=False)
```

```python
import functools

import jax
import jax.numpy as jnp
from jax import lax
from jax.experimental import pallas as pl
from jax.experimental.pallas import tpu as pltpu
from jax.sharding import PartitionSpec as P

MESH = pl.DeviceIdType.MESH
BS = 128
ROWS = 16
INNER = 4
COLS = 8
KEPT = 4
RING = 8
TOP = 32760.0
TINY = 1e-30


DIRECT_TO_1, DIRECT_TO_2 = (6, 7), ()
X_ORDER = Y_ORDER = (0, 1, 2, 3, 7, 6, 5, 4)


def place(index, order):
    found = jnp.int32(0)
    for n, p in enumerate(order):
        found = jnp.where(index == p, n, found)
    return found


def member(n, order):
    found = jnp.int32(0)
    for m, p in enumerate(order):
        found = jnp.where(n == m, p, found)
    return found


def wait_bytes(ref, sem):
    pltpu.make_async_copy(ref, ref, sem).wait()


def kernel(
    a_in, a_slot_in, b_in, b_slot_in, mask_in, out,
    a_slot, b_slot, mask, a_buf, b_buf, a_tab, b_tab, tab_v, tab_s, sel, tx, tx_scale, rx, rx_scale, comp,
    in_sem, own_sem, z_in, x_in, y_in, sib_in, a_recv, b_recv, sib_recv, tab_recv, tab_local,
    a_send, b_send, tab_send, rs_recv, rs_send,
):
    x, z, layer = lax.axis_index("row"), lax.axis_index("col"), lax.axis_index("layer")
    y, core = lax.div(layer, 2), lax.rem(layer, 2)
    other = 1 - core
    twin = y * 2 + other
    sibling = {"layer": twin}
    y_up, y_down = lax.rem(y + 1, RING), lax.rem(y + RING - 1, RING)
    loads = [
        pltpu.make_async_copy(a_slot_in, a_slot, in_sem.at[0]),
        pltpu.make_async_copy(b_slot_in, b_slot, in_sem.at[1]),
        pltpu.make_async_copy(mask_in, mask, in_sem.at[2]),
    ]
    for copy in loads:
        copy.start()

    barrier = pltpu.get_barrier_semaphore()

    def flag(condition):
        return jnp.where(condition, 1, 0)

    def signal(sem, device):
        pl.semaphore_signal(sem, inc=1, device_id=device, device_id_type=MESH)

    at_x, at_y, at_z, at_core = flag(x == 0), flag(y == 0), flag(z == 0), flag(core == 0)
    is_zero = at_x * at_y * at_z * at_core
    x_place, y_place = place(x, X_ORDER), place(y, Y_ORDER)
    z_rank, x_rank, y_rank = z + 8 * is_zero, x_place + 8 * is_zero, y_place + 8 * is_zero
    core_rank = core + 2 * is_zero
    sib_rank = other + 2 * (at_x * at_y * at_z * core)

    def z_peer(p, twin):
        return p + (8 * (at_x * at_y * (core if twin else at_core)) if p == 0 else 0)

    def x_peer(p, twin):
        return X_ORDER.index(p) + (8 * (at_y * at_z * (core if twin else at_core)) if p == 0 else 0)

    def y_peer(p):
        return place(p, Y_ORDER) + 8 * (at_x * at_z * core * flag(p == 0))

    def after(peer, me, fn, *args):
        pl.when(peer > me)(functools.partial(fn, *args))

    def before(peer, me, fn, *args):
        pl.when(peer < me)(functools.partial(fn, *args))

    def ring(place, own_zero, twin_zero):
        spot = lax.rem(place - own_zero + RING, RING)
        turn = twin_zero * flag(place > 0)
        twin_spot = place - turn

        def over(first, end, shift, fn):
            def step(n, carry):
                fn(lax.rem(n + shift, RING))
                return carry

            lax.fori_loop(first, end, step, 0)

        def all_before(fn):
            over(0, spot, own_zero, fn)

        def all_after(fn):
            over(spot + 1, RING, own_zero, fn)

        def twins_before(fn):
            over(is_zero, twin_spot + 8 * is_zero, turn, fn)

        def twins_after(fn):
            over(twin_spot + 1 + 8 * is_zero, RING, turn, fn)

        return all_before, all_after, twins_before, twins_after

    z_before, z_later, z_twins_before, z_twins_later = ring(z, at_x * at_y * at_core, at_x * at_y * core)
    x_before, x_later, x_twins_before, x_twins_later = ring(x_place, at_y * at_z * at_core, at_y * at_z * core)

    def col(p):
        return {"col": p}

    def col_twin(p):
        return {"col": p, "layer": twin}

    def row(n):
        return {"row": member(n, X_ORDER)}

    def row_twin(n):
        return {"row": member(n, X_ORDER), "layer": twin}

    after(sib_rank, core_rank, signal, barrier, sibling)
    for peer in (y_up, y_down):
        after(y_peer(peer), y_rank, signal, barrier, {"layer": peer * 2 + other})
    x_later(lambda n: signal(barrier, row(n)))
    x_twins_later(lambda n: signal(barrier, row_twin(n)))
    z_later(lambda p: signal(barrier, col(p)))
    z_twins_later(lambda p: signal(barrier, col_twin(p)))

    own_a = core * 16 + z * 2
    own_b = core * 8 + x
    own = [
        pltpu.make_async_copy(a_in, a_buf.at[pl.ds(own_a, 2)], own_sem.at[0]),
        pltpu.make_async_copy(b_in, b_buf.at[pl.ds(own_b, 1)], own_sem.at[1]),
    ]
    for copy in own:
        copy.start()
    z_lower = 2 * z - flag(z > 0) * at_x * at_y
    x_lower = 2 * x_place - flag(x > 0) * at_y * at_z
    y_lower = flag(y_peer(y_up) < y_rank) + flag(y_peer(y_down) < y_rank)
    n_lower = jnp.where(is_zero == 1, 4 * (RING - 1), z_lower + x_lower) + y_lower + flag(sib_rank < core_rank)

    @pl.when(n_lower > 0)
    def _():
        pl.semaphore_wait(barrier, n_lower)

    def push(src, dst, send, recv, device):
        pltpu.make_async_remote_copy(
            src_ref=src, dst_ref=dst, send_sem=send, recv_sem=recv, device_id=device, device_id_type=MESH
        ).start()

    def push_a(p):
        push(a_in, a_buf.at[pl.ds(own_a, 2)], a_send, a_recv.at[z], col_twin(p))

    def push_b(device):
        push(b_in, b_buf.at[pl.ds(own_b, 1)], b_send, b_recv.at[x], device)

    def push_a_tab(device):
        row = a_tab.at[core * 8 + z]
        push(row, row, tab_send.at[0], tab_recv.at[0], device)

    def push_b_tab(device):
        row = b_tab.at[core * 8 + x]
        push(row, row, tab_send.at[1], tab_recv.at[1], device)

    group = lax.div(z, 4)
    is_end = flag(z == 0) + flag(z == 3) + flag(z == 4) + flag(z == 7)
    line_of_zero = at_x * at_y * core
    z_inner = {"col": z + 1 - 2 * lax.rem(z, 2), "layer": twin}

    def any_of(index, planes):
        return sum((flag(index == p) for p in planes), jnp.int32(0))

    def push_a_if_direct(p):
        near = flag(lax.div(p, 4) == group)
        end = flag(p == 0) + flag(p == 3) + flag(p == 4) + flag(p == 7)
        extra = flag(p == 1) * any_of(z, DIRECT_TO_1) + flag(p == 2) * any_of(z, DIRECT_TO_2)
        pl.when(near + end + extra > 0)(functools.partial(push_a, p))

    z_twins_before(push_a_if_direct)

    for copy in loads[:2]:
        copy.wait()
    lane = lax.broadcasted_iota(jnp.int32, (1, BS), 1)
    first = jnp.where(lane == core * 64 + a_slot[0], own_a + 1, 0)
    a_tab[core * 8 + z] = jnp.where(lane == core * 64 + a_slot[1], own_a + 2, first)
    b_tab[core * 8 + x] = jnp.where(lane == core * 32 + b_slot[0], own_b + 1, 0)

    z_before(lambda p: push_a_tab(col(p)))
    z_twins_before(lambda p: push_a_tab(col_twin(p)))
    z_before(lambda p: signal(z_in.at[core, z], col(p)))
    z_twins_before(lambda p: signal(z_in.at[core, z], col_twin(p)))
    x_before(lambda n: push_b(row(n)))
    x_before(lambda n: push_b_tab(row(n)))
    x_twins_before(lambda n: push_b_tab(row_twin(n)))
    x_before(lambda n: signal(x_in.at[core, x], row(n)))
    x_twins_before(lambda n: signal(x_in.at[core, x], row_twin(n)))

    before(y_peer(y_up), y_rank, signal, y_in.at[1], {"layer": y_up * 2 + other})
    before(y_peer(y_down), y_rank, signal, y_in.at[0], {"layer": y_down * 2 + other})
    before(sib_rank, core_rank, signal, sib_in, sibling)

    @pl.when(sib_rank > core_rank)
    def _():
        pl.semaphore_wait(sib_in, 1)

    push(a_in, a_buf.at[pl.ds(own_a, 2)], a_send, sib_recv.at[0], sibling)
    push(b_in, b_buf.at[pl.ds(own_b, 1)], b_send, sib_recv.at[1], sibling)
    push_a_tab(sibling)
    push_b_tab(sibling)

    a_buf[32] = jnp.zeros((BS, BS), jnp.bfloat16)
    b_buf[16] = jnp.zeros((BS, BS), jnp.bfloat16)
    comp[KEPT] = jnp.zeros((BS, BS), jnp.float32)

    def x_after(p):
        pl.semaphore_wait(x_in.at[core, p], 1)
        push_b({"row": p})
        push_b_tab({"row": p})

    def x_after_twin(p):
        pl.semaphore_wait(x_in.at[other, p], 1)
        push_b_tab({"row": p, "layer": twin})

    for p in X_ORDER[1:] + (0,):

        @pl.when(p != x)
        def _():
            after(x_peer(p, 0), x_rank, x_after, p)
            after(x_peer(p, 1), x_rank, x_after_twin, p)

    loads[2].wait()

    def pick(t, carry):
        count = jnp.int32(0)
        picks = [jnp.int32(0)] * KEPT
        for j in range(COLS):
            bit = mask[j, t]
            for q in range(KEPT):
                picks[q] = picks[q] + jnp.where(count == q, bit * j, 0)
            count = count + bit
        for q in range(KEPT):
            sel[t, q] = picks[q]
        return carry

    lax.fori_loop(0, ROWS, pick, 0)

    def z_after(p):
        pl.semaphore_wait(z_in.at[core, p], 1)
        push_a_tab({"col": p})

    def z_after_twin(p):
        pl.semaphore_wait(z_in.at[other, p], 1)
        push_a_if_direct(p)
        push_a_tab({"col": p, "layer": twin})

    def offer(peers):
        for p in peers:

            @pl.when(p != z)
            def _():
                after(z_peer(p, 0), z_rank, z_after, p)
                after(z_peer(p, 1), z_rank, z_after_twin, p)

    def share_b():
        for p in range(RING):

            @pl.when(p != x)
            def _():
                block = b_buf.at[pl.ds(core * 8 + p, 1)]
                wait_bytes(block, b_recv.at[p])
                push(block, block, b_send, sib_recv.at[1], sibling)

    def share_a(peers):
        for p in peers:

            @pl.when(p != z)
            def _():
                far = flag(group != p // 4)
                extra = flag(z == 1) * (p in DIRECT_TO_1) + flag(z == 2) * (p in DIRECT_TO_2)
                forwarded = far * (1 - is_end) * (1 - extra)
                blocks = a_buf.at[pl.ds((forwarded * core + (1 - forwarded) * other) * 16 + p * 2, 2)]
                wait_bytes(blocks, a_recv.at[p])

                inwards = is_end * far
                if p in DIRECT_TO_1:
                    inwards = inwards * flag(z != 0)
                if p in DIRECT_TO_2:
                    inwards = inwards * flag(z != 3)

                @pl.when(inwards == 1)
                def _():
                    push(blocks, blocks, a_send, a_recv.at[p], z_inner)

                push(blocks, blocks, a_send, sib_recv.at[0], sibling)

    forwards = (flag(z == 0) + flag(z == 3)) * (1 - line_of_zero)
    offer((1, 2, 3))

    @pl.when(group == 0)
    def _():
        share_b()
        share_a((1, 2, 3))

    offer((4, 5))

    @pl.when(forwards == 1)
    def _():
        share_a((4,))

    offer((6,))

    @pl.when(forwards == 1)
    def _():
        share_a((5,))

    offer((7, 0))

    @pl.when(y_peer(y_up) > y_rank)
    def _():
        pl.semaphore_wait(y_in.at[0], 1)

    @pl.when(y_peer(y_down) > y_rank)
    def _():
        pl.semaphore_wait(y_in.at[1], 1)

    @pl.when(group == 1)
    def _():
        share_b()
        share_a((1, 2, 3))

    @pl.when(forwards == 0)
    def _():
        share_a((4, 5))

    share_a((6, 7, 0))
    wait_bytes(a_tab.at[pl.ds(0, 15)], tab_recv.at[0])
    wait_bytes(b_tab.at[pl.ds(0, 15)], tab_recv.at[1])
    a_at, b_at = jnp.max(a_tab[...], axis=0), jnp.max(b_tab[...], axis=0)
    tab_v[0] = jnp.where(a_at > 0, a_at - 1, 32)
    tab_v[1] = jnp.where(b_at > 0, b_at - 1, 16)
    to_scalars = pltpu.make_async_copy(tab_v, tab_s, tab_local)
    to_scalars.start()
    for copy in own:
        copy.wait()
    to_scalars.wait()
    wait_bytes(a_buf.at[pl.ds(other * 16, 16)], sib_recv.at[0])
    wait_bytes(b_buf.at[pl.ds(other * 8, 8)], sib_recv.at[1])

    slices = [(s, kk) for s in range(2) for kk in range(INNER)]

    def partial(row):
        left = jnp.concatenate([a_buf[tab_s[0, 0, s * 64 + row * INNER + kk]] for s, kk in slices], axis=1)
        sums = []
        for p in range(KEPT // 2):
            right = jnp.concatenate(
                [
                    jnp.concatenate(
                        [b_buf[tab_s[1, 0, s * 32 + kk * COLS + sel[row, 2 * p + q]]] for q in range(2)], axis=1
                    )
                    for s, kk in slices
                ],
                axis=0,
            )
            both = jnp.dot(left, right, preferred_element_type=jnp.float32)
            sums += [both[:, :BS], both[:, BS:]]
        return sums

    def received(slot, q):
        wait_bytes(rx_scale.at[slot, q], rs_recv.at[slot, q, 1])
        wait_bytes(rx.at[slot, q], rs_recv.at[slot, q, 0])
        return rx[slot, q].astype(jnp.int32).astype(jnp.float32) * rx_scale[slot, q]

    def send(slot, q, value, device):
        top = jnp.maximum(jnp.max(jnp.abs(value), axis=0, keepdims=True), TINY)
        tx_scale[slot, q] = top * (1.0 / TOP)
        tx[slot, q] = jnp.round(value * (TOP / top)).astype(jnp.int32).astype(jnp.int16)
        push(tx_scale.at[slot, q], rx_scale.at[slot, q], rs_send.at[1], rs_recv.at[slot, q, 1], device)
        push(tx.at[slot, q], rx.at[slot, q], rs_send.at[0], rs_recv.at[slot, q, 0], device)

    to_up, to_down = {"layer": y_up * 2 + other}, {"layer": y_down * 2 + other}
    up_half, down_half = (0, 1), (2, 3)
    sums = partial(lax.rem(y + 4, RING) * 2 + core)
    for q in up_half:
        send(0, q, sums[q], to_up)
    for q in down_half:
        send(4, q, sums[q], to_down)
    for hop in range(1, 4):
        turned = other if hop % 2 else core
        up = partial(lax.rem(y + 4 - hop, RING) * 2 + turned)
        down = partial(lax.rem(y + 4 + hop, RING) * 2 + turned)
        for q in down_half:
            send(hop, q, up[q] if hop == 1 else up[q] + received(hop - 1, q), to_up)
        for q in up_half:
            send(4 + hop, q, down[q] if hop == 1 else down[q] + received(3 + hop, q), to_down)
        for q in up_half:
            send(hop, q, up[q] + received(hop - 1, q), to_up)
        for q in down_half:
            send(4 + hop, q, down[q] + received(3 + hop, q), to_down)
    sums = partial(layer)
    for q in down_half + up_half:
        comp[q] = sums[q] + received(3, q) + received(7, q)
    count = jnp.int32(0)
    for j in range(COLS):
        bit = mask[j, layer]
        out[:, j * BS : (j + 1) * BS] = comp[jnp.where(bit == 1, count, KEPT)]
        count = count + bit

    wait_bytes(a_buf.at[pl.ds(0, 26)], a_send)
    for plane, more in (
        (0, 4 - len(DIRECT_TO_1)),
        (3, 4 - len(DIRECT_TO_2)),
        (4, 4 + (4 in DIRECT_TO_1) + (4 in DIRECT_TO_2)),
        (5, (5 in DIRECT_TO_1) + (5 in DIRECT_TO_2)),
        (6, (6 in DIRECT_TO_1) + (6 in DIRECT_TO_2)),
        (7, 4 + (7 in DIRECT_TO_1) + (7 in DIRECT_TO_2)),
    ):
        if more:

            @pl.when(z == plane)
            def _():
                wait_bytes(a_buf.at[pl.ds(0, 2 * more)], a_send)

    wait_bytes(b_buf.at[pl.ds(0, 15)], b_send)
    wait_bytes(a_tab.at[pl.ds(0, 15)], tab_send.at[0])
    wait_bytes(b_tab.at[pl.ds(0, 15)], tab_send.at[1])
    wait_bytes(tx.at[pl.ds(0, 7)], rs_send.at[0])
    wait_bytes(tx_scale.at[pl.ds(0, 7)], rs_send.at[1])


def on_device(a_blocks, a_slot, b_blocks, b_slot, c_mask):
    vmem, smem, dma = pltpu.VMEM, pltpu.SMEM, pltpu.SemaphoreType.DMA
    regular = pltpu.SemaphoreType.REGULAR
    operands = (a_blocks, a_slot, b_blocks, b_slot, c_mask.T)
    operands = [operand if operand is b_slot else pltpu.with_memory_space_constraint(operand, pltpu.HBM) for operand in operands]
    return pl.pallas_call(
        kernel,
        out_shape=jax.ShapeDtypeStruct((BS, COLS * BS), jnp.float32),
        in_specs=[pl.BlockSpec(memory_space=pltpu.HBM)] * 5,
        out_specs=pl.BlockSpec(memory_space=vmem),
        scratch_shapes=[
            smem((2,), jnp.int32),
            smem((1,), jnp.int32),
            smem((COLS, ROWS), jnp.int32),
            vmem((33, BS, BS), jnp.bfloat16),
            vmem((17, BS, BS), jnp.bfloat16),
            vmem((2 * RING, 1, BS), jnp.int32),
            vmem((2 * RING, 1, BS), jnp.int32),
            vmem((2, 1, BS), jnp.int32),
            smem((2, 1, BS), jnp.int32),
            smem((ROWS, KEPT), jnp.int32),
            vmem((8, KEPT, BS, BS), jnp.int16),
            vmem((8, KEPT, 1, BS), jnp.float32),
            vmem((8, KEPT, BS, BS), jnp.int16),
            vmem((8, KEPT, 1, BS), jnp.float32),
            vmem((KEPT + 1, BS, BS), jnp.float32),
            dma((3,)),
            dma((2,)),
            regular((2, RING)),
            regular((2, RING)),
            regular((2,)),
            regular(()),
            dma((RING,)),
            dma((RING,)),
            dma((2,)),
            dma((2,)),
            dma(()),
            dma(()),
            dma(()),
            dma((2,)),
            dma((8, KEPT, 2)),
            dma((2,)),
        ],
        compiler_params=pltpu.CompilerParams(
            collective_id=0, has_side_effects=True, vmem_limit_bytes=40 * 1024 * 1024
        ),
    )(*operands)


def solution(mesh):
    in_specs = (
        P(("row", "col", "layer"), None, None),
        P(("row", "col", "layer")),
        P(("row", "col", "layer"), None, None),
        P(("row", "col", "layer")),
        P("row", "col"),
    )
    out_specs = P(("row", "layer"), "col")
    return jax.shard_map(on_device, mesh=mesh, in_specs=in_specs, out_specs=out_specs, check_vma=False)
```
